256 devices in a mesh: rep: 16 (over x_hi, y, core), work: 16 (over x_lo, z).
Axes of the slice: x: 4 (x_hi: 2, x_lo: 2; x = x_hi * 2 + x_lo), y: 4, z: 8, core: 2. Of those that a mesh axis runs over, the one named last changes fastest.
Arguments:
- grads: bfloat16 [8192, 10240], P(('rep', 'work')), may hold values from -6 to 6
- panels: bfloat16 [64, 512, 512], P('work'), may hold values from -0.25 to 0.25
- eigvals: bfloat16 [64, 512], P('work'), may hold values from 0.19921875 to 3
- owner_slot: int32 [56], replicated, may hold values from 0 to 63, as said below
Outputs:
- precond: bfloat16 [8192, 10240], P(('rep', 'work'))
The draws below stay inside these ranges and needn't reach their ends.
Inputs may be any that keep to these rules, and one draw needn't show every extreme that they name: owner_slot holds distinct slot numbers; slot s lies on index s // 4 of work.
All inputs are finite; a program needn't handle non-finite values.
Results may differ from the reference program's by a relative error of at most 0.0054.
Values may be sent and summed in bfloat16 or wider, within the bound.
A program may use at most 64 MiB of HBM per device.

```python
import math
import jax
import jax.numpy as jnp

D = 4096
FF = 10240
FACTOR_ORDER = 512
LAYERS = 2
PANEL_TOTAL = 56
SLOT_NUMBER = 64
N_REP = 16


def draw_owner_slot(key, part):
    key = jax.random.fold_in(key, 11)
    initial_key, second_key = jax.random.split(key)
    inner_product = (jax.random.permutation(initial_key, SLOT_NUMBER - 2) + 1).astype(jnp.int32)
    lookup_table = jnp.concatenate([jnp.array([0, SLOT_NUMBER - 1], jnp.int32), inner_product[:PANEL_TOTAL - 2]])
    placing = jax.random.permutation(second_key, PANEL_TOTAL)
    return lookup_table[placing].astype(jnp.int32)


def block_scale(stream_key, shape, cuts, low, largest):
    def one(position, blocks):
        draws = jax.random.uniform(jax.random.fold_in(jax.random.fold_in(stream_key, 6), position), (blocks,), jnp.float32, low / len(cuts), largest / len(cuts))
        return jnp.repeat(jnp.exp(draws), shape[position] // blocks).reshape((-1,) + (1,) * (len(shape) - position - 1))

    factor_of = one(*cuts[0])
    for cut in cuts[1:]:
        factor_of = factor_of * one(*cut)
    return factor_of


def noise(stream_key, dims, width, bound, cuts=(), kind=jnp.bfloat16):
    level = block_scale(stream_key, dims, cuts, -0.22, 0.18) if cuts else 1.0
    entries = jax.random.normal(stream_key, dims, jnp.float32) * width * level
    return jnp.minimum(jnp.maximum(entries, -bound), bound).astype(kind)


def setup_inputs(seed: int = 0) -> dict:
    seeds = jax.random.split(jax.random.key(seed), 5)
    return {
        "grads": noise(seeds[0], (LAYERS * D, FF), 1.0, 6.0, ((0, 256),)),
        "panels": noise(seeds[1], (SLOT_NUMBER, FACTOR_ORDER, FACTOR_ORDER), FACTOR_ORDER ** -0.5, 0.25, ((0, 16),)),
        "eigvals": jnp.clip(jnp.exp(math.log(3.0) - 2.7119641 * jax.random.uniform(seeds[2], (SLOT_NUMBER, FACTOR_ORDER), jnp.float32) ** block_scale(seeds[2], (SLOT_NUMBER, FACTOR_ORDER), ((0, 16),), -0.2, 0.2)), 0.19921875, 3.0).astype(jnp.bfloat16),
        "owner_slot": draw_owner_slot(jax.random.fold_in(seeds[4], 71), 0),
    }


damping = 0.2


def reference(grads, panels, eigvals, owner_slot):
    right_count = FF // FACTOR_ORDER
    outputs = []
    for group_index in range(N_REP):
        layer_index = group_index * FACTOR_ORDER // D
        first_right = N_REP + layer_index * right_count
        left_panel = panels[owner_slot[group_index]]
        left_values = eigvals[owner_slot[group_index]].astype(jnp.float32)
        block_rows = grads[group_index * FACTOR_ORDER:(group_index + 1) * FACTOR_ORDER]
        rotated = jnp.dot(left_panel.T, block_rows, preferred_element_type=jnp.float32).astype(jnp.bfloat16)
        pieces = []
        for number in range(right_count):
            panel_right = panels[owner_slot[first_right + number]]
            right_values = eigvals[owner_slot[first_right + number]].astype(jnp.float32)
            section = rotated[:, number * FACTOR_ORDER:(number + 1) * FACTOR_ORDER]
            turned = jnp.dot(section, panel_right, preferred_element_type=jnp.float32)
            scaled = (turned / (left_values[:, None] * right_values[None, :] + damping)).astype(jnp.bfloat16)
            pieces.append(jnp.dot(scaled, panel_right.T, preferred_element_type=jnp.float32).astype(jnp.bfloat16))
        restored = jnp.concatenate(pieces, axis=1)
        outputs.append(jnp.dot(left_panel, restored, preferred_element_type=jnp.float32).astype(jnp.bfloat16))
    return jnp.concatenate(outputs, axis=0)
```

```python
import jax
import jax.numpy as jnp
from jax import lax
from jax.experimental import pallas as pl
from jax.experimental.pallas import tpu as pltpu
from jax.sharding import PartitionSpec as P

MESH = pl.DeviceIdType.MESH
N = 512
W = 16
Q = 8
ROWS = 32
RIGHT = 20
LEFT = 16
SLOTS = 4
EXTRA = RIGHT - W
DAMPING = 0.2
BF16 = jnp.bfloat16
F32 = jnp.float32


def partner(w, dx, dz):
    return ((w // 8 + dx) % 2) * 8 + (w % 8 + dz) % 8


def near_first(k):
    return jnp.where(k % 2 == 0, k // 2 + 1, 7 - k // 2)


def extra_home(e):
    return (e // 2) * 8 + (e % 2) * 4 + (e // 2) * 2


def tile(ref, i):
    return ref.at[i // 4, :, pl.ds(pl.multiple_of((i % 4) * 128, 128), 128)]


def kernel(
    owner, grads, panels, eigs, out,
    tiles, eig_all, eig_row, eig_mine, stage_s, stage_p, p_buf, s_buf, rx, tx, xs, us,
    sem_send, sem_t, sem_e, sem_p2, sem_p3, sem_s2, sem_s3, sem_g, sem_o,
):
    r = lax.axis_index("rep")
    w = lax.axis_index("work")
    layer = r // Q
    q = r % Q
    extra = jnp.int32(-1)
    for e in range(EXTRA):
        extra = jnp.where(w == extra_home(e), e, extra)
    has_extra = extra >= 0
    mine = jnp.where(has_extra, extra, 0)

    barrier = pltpu.get_barrier_semaphore()

    def others(body):
        @pl.loop(0, 7)
        def _(k):
            body(partner(w, 0, near_first(k)))

        body(partner(w, 1, 0))

        @pl.loop(0, 7)
        def _(k):
            body(partner(w, 1, near_first(k)))

    def mates(body):
        @pl.loop(1, Q)
        def _(k):
            body((q + k) % Q)

    def greet(t):
        pl.semaphore_signal(barrier, inc=1, device_id={"work": t}, device_id_type=MESH)

    def greet_mate(m):
        pl.semaphore_signal(barrier, inc=1, device_id={"rep": layer * Q + m}, device_id_type=MESH)

    others(greet)
    mates(greet_mate)

    def remote(src, dst, send, recv, **where):
        pltpu.make_async_remote_copy(
            src_ref=src, dst_ref=dst, send_sem=send, recv_sem=recv, device_id=where, device_id_type=MESH
        ).start()

    def local(src, dst, sem):
        pltpu.make_async_copy(src, dst, sem).start()

    def settle(ref, sem):
        pltpu.make_async_copy(ref, ref, sem).wait()

    values = eigs[...].astype(F32)
    for s in range(SLOTS):
        for c in range(4):
            eig_row[4 * s + c : 4 * s + c + 1, :] = values[s : s + 1, c * 128 : (c + 1) * 128]
    eig_mine[...] = eig_row[...].astype(BF16)

    pl.semaphore_wait(barrier, W - 1 + Q - 1)

    def piece_of(i):
        rows = pl.multiple_of(q * 64 + (i // 4) * 16, 16)
        return panels.at[:, pl.ds(rows, 16), pl.ds(pl.multiple_of((i % 4) * 128, 128), 128)]

    def send_tiles(t):
        remote(piece_of(t), tiles.at[pl.ds(w * SLOTS, SLOTS)], sem_send.at[0], sem_t, work=t)
        remote(eig_mine, eig_all.at[w], sem_send.at[1], sem_e, work=t)

    others(send_tiles)
    local(piece_of(w), tiles.at[pl.ds(w * SLOTS, SLOTS)], sem_t)
    local(eig_mine, eig_all.at[w], sem_e)

    def block_of(j):
        return grads.at[:, pl.ds(pl.multiple_of(j * N, N), N)]

    def row_slice(ref, u, k):
        return ref.at[u, pl.ds(pl.multiple_of(k * ROWS, ROWS), ROWS), :]

    def send_rows(t):
        remote(block_of(t), row_slice(rx, 0, w), sem_send.at[2], sem_g.at[0], work=t)

    others(send_rows)
    local(block_of(w), row_slice(rx, 0, w), sem_g.at[0])

    @pl.loop(0, EXTRA)
    def _(k):
        e = (k + w) % EXTRA
        home = extra_home(e)

        @pl.when(home != w)
        def _():
            remote(block_of(W + e), row_slice(rx, 1, w), sem_send.at[3], sem_g.at[1], work=home)

        @pl.when(home == w)
        def _():
            local(block_of(W + e), row_slice(rx, 1, w), sem_g.at[1])

    settle(tiles, sem_t)

    @pl.loop(0, Q)
    def _(m):
        stage_p[m] = tiles[owner[layer * Q + m]]

    def p_tile(k):
        return tile(p_buf.at[k], w)

    def send_p(m):
        remote(stage_p.at[m], p_tile(q), sem_send.at[4], sem_p2, rep=layer * Q + m)

    mates(send_p)
    local(stage_p.at[q], p_tile(q), sem_p2)

    @pl.loop(0, RIGHT)
    def _(j):
        stage_s[j] = tiles[owner[LEFT + layer * RIGHT + j]]

    def send_s(t):
        remote(stage_s.at[t], tile(s_buf.at[0, q], w), sem_send.at[5], sem_s2.at[0], work=t)

    others(send_s)
    local(stage_s.at[w], tile(s_buf.at[0, q], w), sem_s2.at[0])

    @pl.loop(0, EXTRA)
    def _(k):
        e = (k + w) % EXTRA
        home = extra_home(e)

        @pl.when(home != w)
        def _():
            remote(stage_s.at[W + e], tile(s_buf.at[1, q], w), sem_send.at[6], sem_s2.at[1], work=home)

        @pl.when(home == w)
        def _():
            local(stage_s.at[W + e], tile(s_buf.at[1, q], w), sem_s2.at[1])

    def p_share(k):
        return p_buf.at[:, k // 4, :, pl.ds(pl.multiple_of((k % 4) * 128, 128), 128)]

    settle(p_share(w), sem_p2)

    def send_share(t):
        remote(p_share(w), p_share(w), sem_send.at[7], sem_p3, work=t)

    others(send_share)

    settle(s_buf.at[0, q], sem_s2.at[0])

    def send_slab(m):
        remote(s_buf.at[0, q], s_buf.at[0, q], sem_send.at[8], sem_s3.at[0], rep=layer * Q + m)

    mates(send_slab)

    @pl.when(has_extra)
    def _():
        settle(s_buf.at[1, q], sem_s2.at[1])

        def send_slab_extra(m):
            remote(s_buf.at[1, q], s_buf.at[1, q], sem_send.at[9], sem_s3.at[1], rep=layer * Q + m)

        mates(send_slab_extra)

    settle(eig_all, sem_e)

    def values_of(slot):
        whole = eig_all[slot // SLOTS].astype(F32)
        part = slot % SLOTS
        picked = whole[0:4]
        for s in range(1, SLOTS):
            picked = jnp.where(part == s, whole[4 * s : 4 * s + 4], picked)
        return picked

    left = values_of(owner[r])
    columns = []
    for c in range(4):
        columns.append(jnp.transpose(jnp.broadcast_to(left[c : c + 1], (128, 128))))
    left_columns = jnp.concatenate(columns, axis=0)

    others_rows = rx.at[0, pl.ds(0, (W - 1) * ROWS), :]
    settle(others_rows, sem_p3)

    def out_block(j):
        return out.at[:, pl.ds(pl.multiple_of(j * N, N), N)]

    def compute(u, right):
        settle(s_buf.at[u, 0:7], sem_s3.at[u])
        settle(rx.at[u], sem_g.at[u])
        p = p_buf[...].reshape(N, N)
        s = s_buf[u].reshape(N, N)
        for c in range(2):
            cols = slice(c * 256, (c + 1) * 256)
            xs[:, cols] = lax.dot_general(
                p, rx[u, :, cols], (((0,), (0,)), ((), ())), preferred_element_type=F32
            ).astype(BF16)
        for c in range(4):
            cols = slice(c * 128, (c + 1) * 128)
            turned = jnp.dot(xs[...], s[:, cols], preferred_element_type=F32)
            us[:, cols] = (turned / (left_columns * right[c : c + 1] + DAMPING)).astype(BF16)
        for c in range(2):
            cols = slice(c * 256, (c + 1) * 256)
            back = lax.dot_general(
                us[...], s[cols], (((1,), (1,)), ((), ())), preferred_element_type=F32
            ).astype(BF16)
            tx[u, :, cols] = jnp.dot(p, back, preferred_element_type=F32).astype(BF16)

    right0 = values_of(owner[LEFT + layer * RIGHT + w])
    compute(0, right0)

    def send_out(t):
        remote(row_slice(tx, 0, t), out_block(w), sem_send.at[10], sem_o, work=t)

    others(send_out)
    local(row_slice(tx, 0, w), out_block(w), sem_o)

    @pl.when(has_extra)
    def _():
        right1 = values_of(owner[LEFT + layer * RIGHT + W + mine])
        compute(1, right1)

        def send_out_extra(t):
            remote(row_slice(tx, 1, t), out_block(W + mine), sem_send.at[11], sem_o, work=t)

        others(send_out_extra)
        local(row_slice(tx, 1, w), out_block(W + mine), sem_o)

    settle(tiles.at[0 : (W - 1) * SLOTS], sem_send.at[0])
    settle(eig_all.at[0 : W - 1], sem_send.at[1])
    settle(others_rows, sem_send.at[2])
    settle(stage_p.at[0 : Q - 1], sem_send.at[4])
    settle(stage_s.at[0 : W - 1], sem_send.at[5])
    settle(others_rows, sem_send.at[7])
    settle(s_buf.at[0, 0:7], sem_send.at[8])
    settle(others_rows, sem_send.at[10])

    @pl.when(has_extra)
    def _():
        settle(rx.at[0, pl.ds(0, (EXTRA - 1) * ROWS), :], sem_send.at[3])
        settle(stage_s.at[0 : EXTRA - 1], sem_send.at[6])
        settle(s_buf.at[1, 0:7], sem_send.at[9])
        settle(others_rows, sem_send.at[11])

    @pl.when(jnp.logical_not(has_extra))
    def _():
        settle(rx.at[0, pl.ds(0, EXTRA * ROWS), :], sem_send.at[3])
        settle(stage_s.at[0:EXTRA], sem_send.at[6])

    settle(out, sem_o)


def per_device(grads, panels, eigvals, owner_slot):
    return pl.pallas_call(
        kernel,
        out_shape=jax.ShapeDtypeStruct(grads.shape, BF16),
        in_specs=[
            pl.BlockSpec(memory_space=pltpu.SMEM),
            pl.BlockSpec(memory_space=pl.ANY),
            pl.BlockSpec(memory_space=pl.ANY),
            pl.BlockSpec(memory_space=pltpu.VMEM),
        ],
        out_specs=pl.BlockSpec(memory_space=pl.ANY),
        scratch_shapes=[
            pltpu.VMEM((W * SLOTS, 16, 128), BF16),
            pltpu.VMEM((W, 16, 128), BF16),
            pltpu.VMEM((16, 128), F32),
            pltpu.VMEM((16, 128), BF16),
            pltpu.VMEM((RIGHT, 16, 128), BF16),
            pltpu.VMEM((Q, 16, 128), BF16),
            pltpu.VMEM((Q, 4, 16, N), BF16),
            pltpu.VMEM((2, Q, 4, 16, N), BF16),
            pltpu.VMEM((2, N, N), BF16),
            pltpu.VMEM((2, N, N), BF16),
            pltpu.VMEM((N, N), BF16),
            pltpu.VMEM((N, N), BF16),
            pltpu.SemaphoreType.DMA((12,)),
            pltpu.SemaphoreType.DMA,
            pltpu.SemaphoreType.DMA,
            pltpu.SemaphoreType.DMA,
            pltpu.SemaphoreType.DMA,
            pltpu.SemaphoreType.DMA((2,)),
            pltpu.SemaphoreType.DMA((2,)),
            pltpu.SemaphoreType.DMA((2,)),
            pltpu.SemaphoreType.DMA,
        ],
        compiler_params=pltpu.CompilerParams(
            collective_id=0, has_side_effects=True, vmem_limit_bytes=32 * 1024 * 1024
        ),
    )(owner_slot, grads, panels, eigvals)


def solution(mesh):
    return jax.shard_map(
        per_device,
        mesh=mesh,
        in_specs=(P(("rep", "work"), None), P("work", None, None), P("work", None), P()),
        out_specs=P(("rep", "work"), None),
        check_vma=False,
    )
```

```python
import jax
import jax.numpy as jnp
from jax import lax
from jax.experimental import pallas as pl
from jax.experimental.pallas import tpu as pltpu
from jax.sharding import PartitionSpec as P

MESH = pl.DeviceIdType.MESH
N = 512
W = 16
Q = 8
ROWS = 32
RIGHT = 20
LEFT = 16
SLOTS = 4
EXTRA = RIGHT - W
DAMPING = 0.2
BF16 = jnp.bfloat16
F32 = jnp.float32


def partner(w, dx, dz):
    return ((w // 8 + dx) % 2) * 8 + (w % 8 + dz) % 8


def near_first(k):
    return jnp.where(k % 2 == 0, k // 2 + 1, 7 - k // 2)


def extra_home(e, core):
    return (e // 2) * 9 + (e % 2) * 4 + core * 2


def tile(ref, i):
    return ref.at[i // 4, :, pl.ds(pl.multiple_of((i % 4) * 128, 128), 128)]


def kernel(
    owner_hbm, grads_hbm, panels_hbm, eigs_hbm, out,
    owner, grads, panels, eigs,
    tiles, eig_all, eig_row, eig_mine, eig_f32, eig_out, eig_in,
    stage_s, stage_x, stage_p, p_buf, s_buf, rx, tx, xs, us,
    sem_in, sem_send, sem_t, sem_e, sem_p2, sem_p3, sem_p4, sem_x, sem_s2, sem_s3, sem_g, sem_o,
):
    r = lax.axis_index("rep")
    w = lax.axis_index("work")
    layer = r // Q
    q = r % Q
    core = r % 2
    pair = q - core
    keeper = 2 * q
    extra = jnp.int32(-1)
    for e in range(EXTRA):
        extra = jnp.where(w == extra_home(e, core), e, extra)
    has_extra = extra >= 0
    mine = jnp.where(has_extra, extra, 0)

    barrier = pltpu.get_barrier_semaphore()

    def others_z(body):
        @pl.loop(0, 7)
        def _(k):
            body(partner(w, 0, near_first(k)))

    def others(body):
        others_z(body)
        body(partner(w, 1, 0))

        @pl.loop(0, 7)
        def _(k):
            body(partner(w, 1, near_first(k)))

    def mates(body):
        @pl.loop(1, Q)
        def _(k):
            body((q + k) % Q)

    def greet(t):
        pl.semaphore_signal(barrier, inc=1, device_id={"work": t}, device_id_type=MESH)

    def greet_mate(m):
        pl.semaphore_signal(barrier, inc=1, device_id={"rep": layer * Q + m}, device_id_type=MESH)

    others(greet)
    mates(greet_mate)

    def remote(src, dst, send, recv, **where):
        pltpu.make_async_remote_copy(
            src_ref=src, dst_ref=dst, send_sem=send, recv_sem=recv, device_id=where, device_id_type=MESH
        ).start()

    def local(src, dst, sem):
        pltpu.make_async_copy(src, dst, sem).start()

    def settle(ref, sem):
        pltpu.make_async_copy(ref, ref, sem).wait()

    slab = panels_hbm.at[:, pl.ds(pl.multiple_of(q * 64, 64), 64), :]
    local(slab, panels, sem_in.at[0])
    local(eigs_hbm, eigs, sem_in.at[1])
    local(grads_hbm, grads, sem_in.at[2])
    local(owner_hbm, owner, sem_in.at[3])
    settle(eigs, sem_in.at[1])

    values = eigs[...].astype(F32)
    for s in range(SLOTS):
        for c in range(4):
            eig_row[4 * s + c : 4 * s + c + 1, :] = values[s : s + 1, c * 128 : (c + 1) * 128]
    eig_mine[...] = eig_row[...].astype(BF16)

    settle(panels, sem_in.at[0])
    pltpu.make_async_copy(owner_hbm, owner, sem_in.at[3]).wait()
    settle(grads, sem_in.at[2])
    pl.semaphore_wait(barrier, W - 1 + Q - 1)

    def piece_of(i):
        rows = pl.multiple_of((i // 4) * 16, 16)
        return panels.at[:, pl.ds(rows, 16), pl.ds(pl.multiple_of((i % 4) * 128, 128), 128)]

    def send_tiles(t):
        remote(piece_of(t), tiles.at[pl.ds(w * SLOTS, SLOTS)], sem_send.at[0], sem_t, work=t)

    others(send_tiles)
    local(piece_of(w), tiles.at[pl.ds(w * SLOTS, SLOTS)], sem_t)

    @pl.when(w == keeper)
    def _():
        local(eig_mine, eig_all.at[w], sem_e.at[0])

    @pl.when(w != keeper)
    def _():
        remote(eig_mine, eig_all.at[w], sem_send.at[1], sem_e.at[0], work=keeper)

    def block_of(j):
        return grads.at[:, pl.ds(pl.multiple_of(j * N, N), N)]

    def row_slice(ref, u, k):
        return ref.at[u, pl.ds(pl.multiple_of(k * ROWS, ROWS), ROWS), :]

    def send_rows(t):
        remote(block_of(t), row_slice(rx, 0, w), sem_send.at[2], sem_g.at[0], work=t)

    others(send_rows)
    local(block_of(w), row_slice(rx, 0, w), sem_g.at[0])

    @pl.loop(0, EXTRA)
    def _(k):
        e = (k + w) % EXTRA
        home = extra_home(e, core)

        @pl.when(home != w)
        def _():
            remote(block_of(W + e), row_slice(rx, 1, w), sem_send.at[3], sem_g.at[1], work=home)

        @pl.when(home == w)
        def _():
            local(block_of(W + e), row_slice(rx, 1, w), sem_g.at[1])

    settle(tiles, sem_t)

    @pl.loop(0, Q)
    def _(m):
        stage_p[m] = tiles[owner[layer * Q + m]]

    def p_tile(k):
        return tile(p_buf.at[k], w)

    def send_p(m):
        remote(stage_p.at[m], p_tile(q), sem_send.at[4], sem_p2, rep=layer * Q + m)

    mates(send_p)
    local(stage_p.at[q], p_tile(q), sem_p2)

    @pl.loop(0, EXTRA)
    def _(e):
        stage_x[core, e] = tiles[owner[LEFT + layer * RIGHT + W + e]]

    remote(stage_x.at[core], stage_x.at[core], sem_send.at[12], sem_x, rep=layer * Q + pair + 1 - core)

    @pl.loop(0, W)
    def _(j):
        stage_s[j] = tiles[owner[LEFT + layer * RIGHT + j]]

    def send_s(t):
        remote(stage_s.at[t], tile(s_buf.at[0, q], w), sem_send.at[5], sem_s2.at[0], work=t)

    others(send_s)
    local(stage_s.at[w], tile(s_buf.at[0, q], w), sem_s2.at[0])

    settle(stage_x.at[0], sem_x)

    def x_tiles():
        return s_buf.at[1, pl.ds(pair, 2), w // 4, :, pl.ds(pl.multiple_of((w % 4) * 128, 128), 128)]

    @pl.loop(0, EXTRA)
    def _(k):
        e = (k + w) % EXTRA
        home = extra_home(e, core)

        @pl.when(home != w)
        def _():
            remote(stage_x.at[:, e], x_tiles(), sem_send.at[6], sem_s2.at[1], work=home)

        @pl.when(home == w)
        def _():
            local(stage_x.at[:, e], x_tiles(), sem_s2.at[1])

    def p_share(k):
        return p_buf.at[:, k // 4, :, pl.ds(pl.multiple_of((k % 4) * 128, 128), 128)]

    settle(p_share(w), sem_p2)

    def send_share(t):
        remote(p_share(w), p_share(w), sem_send.at[7], sem_p3.at[w % 8], work=t)

    def send_across(k):
        remote(p_share(k), p_share(k), sem_send.at[13], sem_p4, work=partner(w, 1, 0))

    others_z(send_share)
    send_across(w)

    settle(s_buf.at[0, q], sem_s2.at[0])

    def send_slab(m):
        remote(s_buf.at[0, q], s_buf.at[0, q], sem_send.at[8], sem_s3.at[0], rep=layer * Q + m)

    mates(send_slab)

    @pl.when(has_extra)
    def _():
        settle(s_buf.at[1, pl.ds(pair, 2)], sem_s2.at[1])

        @pl.loop(1, 4)
        def _(k):
            both = s_buf.at[1, pl.ds(pair, 2)]
            remote(both, both, sem_send.at[9], sem_s3.at[1], rep=layer * Q + (q + 2 * k) % Q)

    @pl.when(w == keeper)
    def _():
        settle(eig_all, sem_e.at[0])

        def values_of(slot):
            whole = eig_all[slot // SLOTS].astype(F32)
            part = slot % SLOTS
            picked = whole[0:4]
            for s in range(1, SLOTS):
                picked = jnp.where(part == s, whole[4 * s : 4 * s + 4], picked)
            return picked

        eig_f32[0:4, :] = values_of(owner[r])
        eig_f32[12:16, :] = jnp.zeros((4, 128), F32)

        def hand(t):
            second = jnp.int32(0)
            for e in range(EXTRA):
                second = jnp.where(t == extra_home(e, core), e, second)
            eig_f32[4:8, :] = values_of(owner[LEFT + layer * RIGHT + t])
            eig_f32[8:12, :] = values_of(owner[LEFT + layer * RIGHT + W + second])
            eig_out[t] = eig_f32[...].astype(BF16)

        def send_values(t):
            hand(t)
            remote(eig_out.at[t], eig_in, sem_send.at[14], sem_e.at[1], work=t)

        others(send_values)
        hand(w)
        local(eig_out.at[w], eig_in, sem_e.at[1])

    @pl.loop(0, 7)
    def _(k):
        t = partner(w, 0, near_first(k))
        settle(p_share(t), sem_p3.at[t % 8])
        send_across(t)

    settle(eig_in, sem_e.at[1])
    values_in = eig_in[...].astype(F32)
    left = values_in[0:4]
    columns = []
    for c in range(4):
        columns.append(jnp.transpose(jnp.broadcast_to(left[c : c + 1], (128, 128))))
    left_columns = jnp.concatenate(columns, axis=0)

    others_rows = rx.at[0, pl.ds(0, (W - 1) * ROWS), :]
    settle(p_buf.at[:, 0:2], sem_p4)

    def out_block(j):
        return out.at[:, pl.ds(pl.multiple_of(j * N, N), N)]

    def compute(u, right):
        settle(s_buf.at[u, 0 : 7 - u], sem_s3.at[u])
        settle(rx.at[u], sem_g.at[u])
        p = p_buf[...].reshape(N, N)
        s = s_buf[u].reshape(N, N)
        for c in range(2):
            cols = slice(c * 256, (c + 1) * 256)
            xs[:, cols] = lax.dot_general(
                p, rx[u, :, cols], (((0,), (0,)), ((), ())), preferred_element_type=F32
            ).astype(BF16)
        for c in range(4):
            cols = slice(c * 128, (c + 1) * 128)
            turned = jnp.dot(xs[...], s[:, cols], preferred_element_type=F32)
            us[:, cols] = (turned / (left_columns * right[c : c + 1] + DAMPING)).astype(BF16)
        for c in range(2):
            cols = slice(c * 256, (c + 1) * 256)
            back = lax.dot_general(
                us[...], s[cols], (((1,), (1,)), ((), ())), preferred_element_type=F32
            ).astype(BF16)
            tx[u, :, cols] = jnp.dot(p, back, preferred_element_type=F32).astype(BF16)

    compute(0, values_in[4:8])

    def send_out(t):
        remote(row_slice(tx, 0, t), out_block(w), sem_send.at[10], sem_o, work=t)

    others(send_out)
    local(row_slice(tx, 0, w), out_block(w), sem_o)

    @pl.when(has_extra)
    def _():
        compute(1, values_in[8:12])

        def send_out_extra(t):
            remote(row_slice(tx, 1, t), out_block(W + mine), sem_send.at[11], sem_o, work=t)

        others(send_out_extra)
        local(row_slice(tx, 1, w), out_block(W + mine), sem_o)

    settle(tiles.at[0 : (W - 1) * SLOTS], sem_send.at[0])

    @pl.when(w == keeper)
    def _():
        settle(eig_out.at[0 : W - 1], sem_send.at[14])

    @pl.when(w != keeper)
    def _():
        settle(eig_mine, sem_send.at[1])

    settle(others_rows, sem_send.at[2])
    settle(stage_p.at[0 : Q - 1], sem_send.at[4])
    settle(stage_s.at[0 : W - 1], sem_send.at[5])
    settle(rx.at[0, pl.ds(0, 7 * ROWS), :], sem_send.at[7])
    settle(stage_x.at[0], sem_send.at[12])
    settle(p_buf.at[:, 0:2], sem_send.at[13])
    settle(s_buf.at[0, 0:7], sem_send.at[8])
    settle(others_rows, sem_send.at[10])

    @pl.when(has_extra)
    def _():
        settle(rx.at[0, pl.ds(0, (EXTRA - 1) * ROWS), :], sem_send.at[3])
        settle(stage_s.at[0 : 2 * (EXTRA - 1)], sem_send.at[6])
        settle(s_buf.at[1, 0:6], sem_send.at[9])
        settle(others_rows, sem_send.at[11])

    @pl.when(jnp.logical_not(has_extra))
    def _():
        settle(rx.at[0, pl.ds(0, EXTRA * ROWS), :], sem_send.at[3])
        settle(stage_s.at[0 : 2 * EXTRA], sem_send.at[6])

    settle(out, sem_o)


def per_device(grads, panels, eigvals, owner_slot):
    return pl.pallas_call(
        kernel,
        out_shape=jax.ShapeDtypeStruct(grads.shape, BF16),
        in_specs=[
            pl.BlockSpec(memory_space=pltpu.HBM),
            pl.BlockSpec(memory_space=pltpu.HBM),
            pl.BlockSpec(memory_space=pltpu.HBM),
            pl.BlockSpec(memory_space=pltpu.HBM),
        ],
        out_specs=pl.BlockSpec(memory_space=pl.ANY),
        scratch_shapes=[
            pltpu.SMEM(owner_slot.shape, jnp.int32),
            pltpu.VMEM(grads.shape, BF16),
            pltpu.VMEM((SLOTS, N // Q, N), BF16),
            pltpu.VMEM(eigvals.shape, BF16),
            pltpu.VMEM((W * SLOTS, 16, 128), BF16),
            pltpu.VMEM((W, 16, 128), BF16),
            pltpu.VMEM((16, 128), F32),
            pltpu.VMEM((16, 128), BF16),
            pltpu.VMEM((16, 128), F32),
            pltpu.VMEM((W, 16, 128), BF16),
            pltpu.VMEM((16, 128), BF16),
            pltpu.VMEM((W, 16, 128), BF16),
            pltpu.VMEM((2, EXTRA, 16, 128), BF16),
            pltpu.VMEM((Q, 16, 128), BF16),
            pltpu.VMEM((Q, 4, 16, N), BF16),
            pltpu.VMEM((2, Q, 4, 16, N), BF16),
            pltpu.VMEM((2, N, N), BF16),
            pltpu.VMEM((2, N, N), BF16),
            pltpu.VMEM((N, N), BF16),
            pltpu.VMEM((N, N), BF16),
            pltpu.SemaphoreType.DMA((4,)),
            pltpu.SemaphoreType.DMA((15,)),
            pltpu.SemaphoreType.DMA,
            pltpu.SemaphoreType.DMA((2,)),
            pltpu.SemaphoreType.DMA,
            pltpu.SemaphoreType.DMA((8,)),
            pltpu.SemaphoreType.DMA,
            pltpu.SemaphoreType.DMA,
            pltpu.SemaphoreType.DMA((2,)),
            pltpu.SemaphoreType.DMA((2,)),
            pltpu.SemaphoreType.DMA((2,)),
            pltpu.SemaphoreType.DMA,
        ],
        compiler_params=pltpu.CompilerParams(
            collective_id=0, has_side_effects=True, vmem_limit_bytes=32 * 1024 * 1024
        ),
    )(owner_slot, grads, panels, eigvals)


def solution(mesh):
    return jax.shard_map(
        per_device,
        mesh=mesh,
        in_specs=(P(("rep", "work"), None), P("work", None, None), P("work", None), P()),
        out_specs=P(("rep", "work"), None),
        check_vma=False,
    )
```

```python
import jax
import jax.numpy as jnp
from jax import lax
from jax.experimental import pallas as pl
from jax.experimental.pallas import tpu as pltpu
from jax.sharding import PartitionSpec as P

MESH = pl.DeviceIdType.MESH
N = 512
W = 16
Q = 8
ROWS = 32
RIGHT = 20
LEFT = 16
SLOTS = 4
EXTRA = RIGHT - W
DAMPING = 0.2
BF16 = jnp.bfloat16
F32 = jnp.float32


def partner(w, dx, dz):
    return ((w // 8 + dx) % 2) * 8 + (w % 8 + dz) % 8


def near_first(k):
    return jnp.where(k % 2 == 0, k // 2 + 1, 7 - k // 2)


def extra_home(e, core):
    return (e // 2) * 9 + (e % 2) * 4 + core * 2


def tile(ref, i):
    return ref.at[i // 4, :, pl.ds(pl.multiple_of((i % 4) * 128, 128), 128)]


def kernel(
    owner_hbm, grads_hbm, panels_hbm, eigs_hbm, out,
    owner, grads, panels, eigs,
    tiles, eig_all, eig_mine, eig_f32, eig_out, eig_in,
    stage_s, stage_x, stage_p, p_buf, s_buf, rx, tx, xs, us,
    sem_in, sem_send, sem_t, sem_e, sem_p2, sem_p3, sem_p4, sem_x, sem_s2, sem_s3, sem_g, sem_o,
):
    r = lax.axis_index("rep")
    w = lax.axis_index("work")
    layer = r // Q
    q = r % Q
    core = r % 2
    pair = q - core
    keeper = 2 * q
    extra = jnp.int32(-1)
    for e in range(EXTRA):
        extra = jnp.where(w == extra_home(e, core), e, extra)
    has_extra = extra >= 0
    mine = jnp.where(has_extra, extra, 0)

    barrier = pltpu.get_barrier_semaphore()

    def others_z(body):
        @pl.loop(0, 7)
        def _(k):
            body(partner(w, 0, near_first(k)))

    def others_x(body):
        @pl.loop(0, 7)
        def _(k):
            body(partner(w, 1, near_first(k)))

    def others(body):
        others_z(body)
        body(partner(w, 1, 0))
        others_x(body)

    def mates(body):
        @pl.loop(1, Q)
        def _(k):
            body((q + k) % Q)

    def greet(t):
        pl.semaphore_signal(barrier, inc=1, device_id={"work": t}, device_id_type=MESH)

    def greet_mate(m):
        pl.semaphore_signal(barrier, inc=1, device_id={"rep": layer * Q + m}, device_id_type=MESH)

    others(greet)
    mates(greet_mate)

    def remote(src, dst, send, recv, **where):
        pltpu.make_async_remote_copy(
            src_ref=src, dst_ref=dst, send_sem=send, recv_sem=recv, device_id=where, device_id_type=MESH
        ).start()

    def local(src, dst, sem):
        pltpu.make_async_copy(src, dst, sem).start()

    def settle(ref, sem):
        pltpu.make_async_copy(ref, ref, sem).wait()

    slab = panels_hbm.at[:, pl.ds(pl.multiple_of(q * 64, 64), 64), :]
    local(slab, panels, sem_in.at[0])
    local(eigs_hbm, eigs, sem_in.at[1])
    local(grads_hbm, grads, sem_in.at[2])
    local(owner_hbm, owner, sem_in.at[3])
    settle(panels, sem_in.at[0])
    pl.semaphore_wait(barrier, W - 1 + Q - 1)

    def piece_of(i):
        rows = pl.multiple_of((i // 4) * 16, 16)
        return panels.at[:, pl.ds(rows, 16), pl.ds(pl.multiple_of((i % 4) * 128, 128), 128)]

    def tiles_out():
        def send_tiles(t):
            remote(piece_of(t), tiles.at[pl.ds(w * SLOTS, SLOTS)], sem_send.at[0], sem_t, work=t)

        others(send_tiles)
        local(piece_of(w), tiles.at[pl.ds(w * SLOTS, SLOTS)], sem_t)

    def values_out():
        settle(eigs, sem_in.at[1])

        values = eigs[...].astype(F32)
        for s in range(SLOTS):
            for c in range(4):
                eig_f32[c : c + 1, :] = values[s : s + 1, c * 128 : (c + 1) * 128]
            eig_mine[s] = eig_f32[...].astype(BF16)

        @pl.when(w == keeper)
        def _():
            local(eig_mine, eig_all.at[pl.ds(w * SLOTS, SLOTS)], sem_e.at[0])

        @pl.when(w != keeper)
        def _():
            remote(eig_mine, eig_all.at[pl.ds(w * SLOTS, SLOTS)], sem_send.at[1], sem_e.at[0], work=keeper)

    def block_of(j):
        return grads.at[:, pl.ds(pl.multiple_of(j * N, N), N)]

    def row_slice(ref, u, k):
        return ref.at[u, pl.ds(pl.multiple_of(k * ROWS, ROWS), ROWS), :]

    def send_rows(t):
        remote(block_of(t), row_slice(rx, 0, w), sem_send.at[2], sem_g.at[0], work=t)

    def rows_ready():
        settle(grads, sem_in.at[2])
        rows_own()

    def rows_own():
        local(block_of(w), row_slice(rx, 0, w), sem_g.at[0])

    def rows_to(dx, *steps):
        for dz in steps:
            send_rows(partner(w, dx, dz))

    def rows_extra(a, b):
        @pl.loop(a, b)
        def _(k):
            e = (k + w) % EXTRA
            home = extra_home(e, core)

            @pl.when(home != w)
            def _():
                remote(block_of(W + e), row_slice(rx, 1, w), sem_send.at[3], sem_g.at[1], work=home)

            @pl.when(home == w)
            def _():
                local(block_of(W + e), row_slice(rx, 1, w), sem_g.at[1])

    def p_tile(k):
        return tile(p_buf.at[k], w)

    def left_tiles():
        settle(tiles, sem_t)
        pltpu.make_async_copy(owner_hbm, owner, sem_in.at[3]).wait()

        @pl.loop(0, Q)
        def _(m):
            stage_p[m] = tiles[owner[layer * Q + m]]

        def send_p(m):
            remote(stage_p.at[m], p_tile(q), sem_send.at[4], sem_p2, rep=layer * Q + m)

        mates(send_p)
        local(stage_p.at[q], p_tile(q), sem_p2)

    def extra_tiles_pair():
        @pl.loop(0, EXTRA)
        def _(e):
            stage_x[core, e] = tiles[owner[LEFT + layer * RIGHT + W + e]]

        remote(stage_x.at[core], stage_x.at[core], sem_send.at[12], sem_x, rep=layer * Q + pair + 1 - core)

    def right_tiles():
        @pl.loop(0, W)
        def _(j):
            stage_s[j] = tiles[owner[LEFT + layer * RIGHT + j]]

        def send_s(t):
            remote(stage_s.at[t], tile(s_buf.at[0, q], w), sem_send.at[5], sem_s2.at[0], work=t)

        others(send_s)
        local(stage_s.at[w], tile(s_buf.at[0, q], w), sem_s2.at[0])

    def extra_tiles():
        settle(stage_x.at[0], sem_x)

        def x_tiles():
            return s_buf.at[1, pl.ds(pair, 2), w // 4, :, pl.ds(pl.multiple_of((w % 4) * 128, 128), 128)]

        @pl.loop(0, EXTRA)
        def _(k):
            e = (k + w) % EXTRA
            home = extra_home(e, core)

            @pl.when(home != w)
            def _():
                remote(stage_x.at[:, e], x_tiles(), sem_send.at[6], sem_s2.at[1], work=home)

            @pl.when(home == w)
            def _():
                local(stage_x.at[:, e], x_tiles(), sem_s2.at[1])

    def p_share(k):
        return p_buf.at[:, k // 4, :, pl.ds(pl.multiple_of((k % 4) * 128, 128), 128)]

    def send_across(k):
        remote(p_share(k), p_share(k), sem_send.at[13], sem_p4, work=partner(w, 1, 0))

    def left_shares():
        settle(p_share(w), sem_p2)

        def send_share(t):
            remote(p_share(w), p_share(w), sem_send.at[7], sem_p3.at[w % 8], work=t)

        others_z(send_share)
        send_across(w)

    def right_slabs():
        settle(s_buf.at[0, q], sem_s2.at[0])

        def send_slab(m):
            remote(s_buf.at[0, q], s_buf.at[0, q], sem_send.at[8], sem_s3.at[0], rep=layer * Q + m)

        mates(send_slab)

    def extra_slabs():
        @pl.when(has_extra)
        def _():
            settle(s_buf.at[1, pl.ds(pair, 2)], sem_s2.at[1])

            @pl.loop(1, 4)
            def _(k):
                both = s_buf.at[1, pl.ds(pair, 2)]
                remote(both, both, sem_send.at[9], sem_s3.at[1], rep=layer * Q + (q + 2 * k) % Q)

    def hand_values():
        @pl.when(w == keeper)
        def _():
            settle(eig_all, sem_e.at[0])

            def hand(t):
                second = jnp.int32(0)
                for e in range(EXTRA):
                    second = jnp.where(t == extra_home(e, core), e, second)
                eig_out[t, 0] = eig_all[owner[r]]
                eig_out[t, 1] = eig_all[owner[LEFT + layer * RIGHT + t]]
                eig_out[t, 2] = eig_all[owner[LEFT + layer * RIGHT + W + second]]

            def send_values(t):
                hand(t)
                remote(eig_out.at[t], eig_in, sem_send.at[14], sem_e.at[1], work=t)

            others(send_values)
            hand(w)
            local(eig_out.at[w], eig_in, sem_e.at[1])

    def pass_on():
        @pl.loop(0, 7)
        def _(k):
            t = partner(w, 0, near_first(k))
            settle(p_share(t), sem_p3.at[t % 8])
            send_across(t)

    tiles_out()
    rows_ready()
    rows_extra(0, 4)

    @pl.when(core == 0)
    def _():
        rows_to(1, 0)
        rows_to(1, 1, 7)
        rows_to(1, 2, 6)
        rows_to(1, 3, 5)
        rows_to(1, 4)
        rows_to(0, 1, 7)
        rows_to(0, 2, 6)
        rows_to(0, 3, 5)
        rows_to(0, 4)

    values_out()
    left_tiles()
    extra_tiles_pair()
    right_tiles()
    extra_tiles()
    left_shares()
    right_slabs()
    extra_slabs()
    hand_values()

    @pl.when(core == 1)
    def _():
        rows_to(1, 0)
        rows_to(1, 1, 7)
        rows_to(1, 2, 6)
        rows_to(1, 3, 5)
        rows_to(1, 4)
        rows_to(0, 1, 7)
        rows_to(0, 2, 6)
        rows_to(0, 3, 5)
        rows_to(0, 4)

    pass_on()

    settle(eig_in, sem_e.at[1])
    left = eig_in[0].astype(F32)
    columns = []
    for c in range(4):
        columns.append(jnp.transpose(jnp.broadcast_to(left[c : c + 1], (128, 128))))
    left_columns = jnp.concatenate(columns, axis=0)

    others_rows = rx.at[0, pl.ds(0, (W - 1) * ROWS), :]
    settle(p_buf.at[:, 0:2], sem_p4)

    def compute(u, j):
        settle(rx.at[u], sem_g.at[u])
        p = p_buf[...].reshape(N, N)
        halves = [slice(c * 256, (c + 1) * 256) for c in range(2)]
        for cols in halves:
            xs[:, cols] = lax.dot_general(
                p, rx[u, :, cols], (((0,), (0,)), ((), ())), preferred_element_type=F32
            ).astype(BF16)
        settle(s_buf.at[u, 0 : 7 - u], sem_s3.at[u])
        s = s_buf[u].reshape(N, N)
        right = eig_in[1 + u].astype(F32)
        for c in range(4):
            cols = slice(c * 128, (c + 1) * 128)
            turned = jnp.dot(xs[...], s[:, cols], preferred_element_type=F32)
            us[:, cols] = (turned / (left_columns * right[c : c + 1] + DAMPING)).astype(BF16)
        for c, cols in enumerate(halves):
            back = lax.dot_general(
                us[...], s[cols], (((1,), (1,)), ((), ())), preferred_element_type=F32
            ).astype(BF16)
            tx[u, c] = jnp.dot(p, back, preferred_element_type=F32).astype(BF16)

            def send_out(t):
                remote(own_rows(t), out_block(t), sem_send.at[10 + u], sem_o, work=t)

            def own_rows(t):
                return tx.at[u, c, pl.ds(pl.multiple_of(t * ROWS, ROWS), ROWS), :]

            def out_block(t):
                return out.at[:, pl.ds(pl.multiple_of(j * N + c * 256, 256), 256)]

            others(send_out)
            local(own_rows(w), out_block(w), sem_o)

    compute(0, w)

    @pl.when(has_extra)
    def _():
        compute(1, W + mine)

    settle(tiles.at[0 : (W - 1) * SLOTS], sem_send.at[0])

    @pl.when(w == keeper)
    def _():
        settle(eig_out.at[0 : W - 1], sem_send.at[14])

    @pl.when(w != keeper)
    def _():
        settle(eig_mine, sem_send.at[1])

    settle(stage_p.at[0 : Q - 1], sem_send.at[4])
    settle(stage_s.at[0 : W - 1], sem_send.at[5])
    settle(rx.at[0, pl.ds(0, 7 * ROWS), :], sem_send.at[7])
    settle(stage_x.at[0], sem_send.at[12])
    settle(p_buf.at[:, 0:2], sem_send.at[13])
    settle(s_buf.at[0, 0:7], sem_send.at[8])
    settle(others_rows, sem_send.at[2])
    settle(others_rows, sem_send.at[10])

    @pl.when(has_extra)
    def _():
        settle(rx.at[0, pl.ds(0, (EXTRA - 1) * ROWS), :], sem_send.at[3])
        settle(stage_s.at[0 : 2 * (EXTRA - 1)], sem_send.at[6])
        settle(s_buf.at[1, 0:6], sem_send.at[9])
        settle(others_rows, sem_send.at[11])

    @pl.when(jnp.logical_not(has_extra))
    def _():
        settle(rx.at[0, pl.ds(0, EXTRA * ROWS), :], sem_send.at[3])
        settle(stage_s.at[0 : 2 * EXTRA], sem_send.at[6])

    settle(out, sem_o)


def per_device(grads, panels, eigvals, owner_slot):
    return pl.pallas_call(
        kernel,
        out_shape=jax.ShapeDtypeStruct(grads.shape, BF16),
        in_specs=[
            pl.BlockSpec(memory_space=pltpu.HBM),
            pl.BlockSpec(memory_space=pltpu.HBM),
            pl.BlockSpec(memory_space=pltpu.HBM),
            pl.BlockSpec(memory_space=pltpu.HBM),
        ],
        out_specs=pl.BlockSpec(memory_space=pl.ANY),
        scratch_shapes=[
            pltpu.SMEM(owner_slot.shape, jnp.int32),
            pltpu.VMEM(grads.shape, BF16),
            pltpu.VMEM((SLOTS, N // Q, N), BF16),
            pltpu.VMEM(eigvals.shape, BF16),
            pltpu.VMEM((W * SLOTS, 16, 128), BF16),
            pltpu.VMEM((W * SLOTS, 16, 128), BF16),
            pltpu.VMEM((SLOTS, 16, 128), BF16),
            pltpu.VMEM((16, 128), F32),
            pltpu.VMEM((W, 3, 16, 128), BF16),
            pltpu.VMEM((3, 16, 128), BF16),
            pltpu.VMEM((W, 16, 128), BF16),
            pltpu.VMEM((2, EXTRA, 16, 128), BF16),
            pltpu.VMEM((Q, 16, 128), BF16),
            pltpu.VMEM((Q, 4, 16, N), BF16),
            pltpu.VMEM((2, Q, 4, 16, N), BF16),
            pltpu.VMEM((2, N, N), BF16),
            pltpu.VMEM((2, 2, N, N // 2), BF16),
            pltpu.VMEM((N, N), BF16),
            pltpu.VMEM((N, N), BF16),
            pltpu.SemaphoreType.DMA((4,)),
            pltpu.SemaphoreType.DMA((15,)),
            pltpu.SemaphoreType.DMA,
            pltpu.SemaphoreType.DMA((2,)),
            pltpu.SemaphoreType.DMA,
            pltpu.SemaphoreType.DMA((8,)),
            pltpu.SemaphoreType.DMA,
            pltpu.SemaphoreType.DMA,
            pltpu.SemaphoreType.DMA((2,)),
            pltpu.SemaphoreType.DMA((2,)),
            pltpu.SemaphoreType.DMA((2,)),
            pltpu.SemaphoreType.DMA,
        ],
        compiler_params=pltpu.CompilerParams(
            collective_id=0, has_side_effects=True, vmem_limit_bytes=32 * 1024 * 1024
        ),
    )(*[pltpu.with_memory_space_constraint(x, pltpu.HBM) for x in (owner_slot, grads, panels, eigvals)])


def solution(mesh):
    return jax.shard_map(
        per_device,
        mesh=mesh,
        in_specs=(P(("rep", "work"), None), P("work", None, None), P("work", None), P()),
        out_specs=P(("rep", "work"), None),
        check_vma=False,
    )
```

```python
import jax
import jax.numpy as jnp
from jax import lax
from jax.experimental import pallas as pl
from jax.experimental.pallas import tpu as pltpu
from jax.sharding import PartitionSpec as P

MESH = pl.DeviceIdType.MESH
N = 512
W = 16
Q = 8
ROWS = 32
RIGHT = 20
LEFT = 16
SLOTS = 4
EXTRA = RIGHT - W
DAMPING = 0.2
BF16 = jnp.bfloat16
F32 = jnp.float32


def partner(w, dx, dz):
    return ((w // 8 + dx) % 2) * 8 + (w % 8 + dz) % 8


def near_first(k):
    return jnp.where(k % 2 == 0, k // 2 + 1, 7 - k // 2)


def extra_home(e, core):
    return (e // 2) * 9 + (e % 2) * 4 + core * 2


def tile(ref, i):
    return ref.at[i // 4, :, pl.ds(pl.multiple_of((i % 4) * 128, 128), 128)]


def kernel(
    owner_hbm, grads_hbm, panels_hbm, eigs_hbm, out,
    owner, grads, panels, eigs,
    tiles, eig_all, eig_mine, eig_f32, eig_out, eig_in,
    stage_s, stage_x, stage_p, p_buf, s_buf, rx, tx, xs, us,
    sem_in, sem_send, sem_t, sem_e, sem_p2, sem_p3, sem_p4, sem_x, sem_s2, sem_s3, sem_g, sem_o,
):
    r = lax.axis_index("rep")
    w = lax.axis_index("work")
    layer = r // Q
    q = r % Q
    core = r % 2
    pair = q - core
    keeper = 2 * q
    extra = jnp.int32(-1)
    for e in range(EXTRA):
        extra = jnp.where(w == extra_home(e, core), e, extra)
    has_extra = extra >= 0
    mine = jnp.where(has_extra, extra, 0)

    barrier = pltpu.get_barrier_semaphore()

    def others_z(body):
        @pl.loop(0, 7)
        def _(k):
            body(partner(w, 0, near_first(k)))

    def others_x(body):
        @pl.loop(0, 7)
        def _(k):
            body(partner(w, 1, near_first(k)))

    def others(body):
        others_z(body)
        body(partner(w, 1, 0))
        others_x(body)

    def mates(body):
        @pl.loop(1, Q)
        def _(k):
            body((q + k) % Q)

    def greet(t):
        pl.semaphore_signal(barrier, inc=1, device_id={"work": t}, device_id_type=MESH)

    def greet_mate(m):
        pl.semaphore_signal(barrier, inc=1, device_id={"rep": layer * Q + m}, device_id_type=MESH)

    others(greet)
    mates(greet_mate)

    def remote(src, dst, send, recv, **where):
        pltpu.make_async_remote_copy(
            src_ref=src, dst_ref=dst, send_sem=send, recv_sem=recv, device_id=where, device_id_type=MESH
        ).start()

    def local(src, dst, sem):
        pltpu.make_async_copy(src, dst, sem).start()

    def settle(ref, sem):
        pltpu.make_async_copy(ref, ref, sem).wait()

    slab = panels_hbm.at[:, pl.ds(pl.multiple_of(q * 64, 64), 64), :]
    local(slab, panels, sem_in.at[0])
    local(eigs_hbm, eigs, sem_in.at[1])
    local(grads_hbm, grads, sem_in.at[2])
    local(owner_hbm, owner, sem_in.at[3])
    settle(panels, sem_in.at[0])
    pl.semaphore_wait(barrier, W - 1 + Q - 1)

    def piece_of(i):
        rows = pl.multiple_of((i // 4) * 16, 16)
        return panels.at[:, pl.ds(rows, 16), pl.ds(pl.multiple_of((i % 4) * 128, 128), 128)]

    def tiles_out():
        def send_tiles(t):
            remote(piece_of(t), tiles.at[pl.ds(w * SLOTS, SLOTS)], sem_send.at[0], sem_t, work=t)

        others(send_tiles)
        local(piece_of(w), tiles.at[pl.ds(w * SLOTS, SLOTS)], sem_t)

    def values_out():
        settle(eigs, sem_in.at[1])

        values = eigs[...].astype(F32)
        for s in range(SLOTS):
            for c in range(4):
                eig_f32[c : c + 1, :] = values[s : s + 1, c * 128 : (c + 1) * 128]
            eig_mine[s] = eig_f32[...].astype(BF16)

        @pl.when(w == keeper)
        def _():
            local(eig_mine, eig_all.at[pl.ds(w * SLOTS, SLOTS)], sem_e.at[0])

        @pl.when(w != keeper)
        def _():
            remote(eig_mine, eig_all.at[pl.ds(w * SLOTS, SLOTS)], sem_send.at[1], sem_e.at[0], work=keeper)

    def block_of(j):
        return grads.at[:, pl.ds(pl.multiple_of(j * N, N), N)]

    def row_slice(ref, u, k):
        return ref.at[u, pl.ds(pl.multiple_of(k * ROWS, ROWS), ROWS), :]

    def send_rows(t):
        remote(block_of(t), row_slice(rx, 0, w), sem_send.at[2], sem_g.at[0], work=t)

    def rows_ready():
        settle(grads, sem_in.at[2])
        rows_own()

    def rows_own():
        local(block_of(w), row_slice(rx, 0, w), sem_g.at[0])

    def rows_to(dx, *steps):
        for dz in steps:
            send_rows(partner(w, dx, dz))

    def rows_extra(a, b):
        @pl.loop(a, b)
        def _(k):
            e = (k + w) % EXTRA
            home = extra_home(e, core)

            @pl.when(home != w)
            def _():
                remote(block_of(W + e), row_slice(rx, 1, w), sem_send.at[3], sem_g.at[1], work=home)

            @pl.when(home == w)
            def _():
                local(block_of(W + e), row_slice(rx, 1, w), sem_g.at[1])

    def p_tile(k):
        return tile(p_buf.at[k], w)

    def left_tiles():
        settle(tiles, sem_t)
        pltpu.make_async_copy(owner_hbm, owner, sem_in.at[3]).wait()

        @pl.loop(0, Q)
        def _(m):
            stage_p[m] = tiles[owner[layer * Q + m]]

        def send_p(m):
            remote(stage_p.at[m], p_tile(q), sem_send.at[4], sem_p2, rep=layer * Q + m)

        mates(send_p)
        local(stage_p.at[q], p_tile(q), sem_p2)

    def extra_tiles_pair():
        @pl.loop(0, EXTRA)
        def _(e):
            stage_x[core, e] = tiles[owner[LEFT + layer * RIGHT + W + e]]

        remote(stage_x.at[core], stage_x.at[core], sem_send.at[12], sem_x, rep=layer * Q + pair + 1 - core)

    def right_tiles():
        @pl.loop(0, W)
        def _(j):
            stage_s[j] = tiles[owner[LEFT + layer * RIGHT + j]]

        def send_s(t):
            remote(stage_s.at[t], tile(s_buf.at[0, q], w), sem_send.at[5], sem_s2.at[0], work=t)

        others(send_s)
        local(stage_s.at[w], tile(s_buf.at[0, q], w), sem_s2.at[0])

    def extra_tiles():
        settle(stage_x.at[0], sem_x)

        def x_tiles():
            return s_buf.at[1, pl.ds(pair, 2), w // 4, :, pl.ds(pl.multiple_of((w % 4) * 128, 128), 128)]

        @pl.loop(0, EXTRA)
        def _(k):
            e = (k + w) % EXTRA
            home = extra_home(e, core)

            @pl.when(home != w)
            def _():
                remote(stage_x.at[:, e], x_tiles(), sem_send.at[6], sem_s2.at[1], work=home)

            @pl.when(home == w)
            def _():
                local(stage_x.at[:, e], x_tiles(), sem_s2.at[1])

    def p_share(k):
        return p_buf.at[:, k // 4, :, pl.ds(pl.multiple_of((k % 4) * 128, 128), 128)]

    def send_across(k):
        remote(p_share(k), p_share(k), sem_send.at[13], sem_p4, work=partner(w, 1, 0))

    def left_shares():
        settle(p_share(w), sem_p2)

        def send_share(t):
            remote(p_share(w), p_share(w), sem_send.at[7], sem_p3.at[w % 8], work=t)

        others_z(send_share)
        send_across(w)

    def right_slabs():
        settle(s_buf.at[0, q], sem_s2.at[0])

        def send_slab(m):
            remote(s_buf.at[0, q], s_buf.at[0, q], sem_send.at[8], sem_s3.at[0], rep=layer * Q + m)

        mates(send_slab)

    def extra_slabs():
        @pl.when(has_extra)
        def _():
            settle(s_buf.at[1, pl.ds(pair, 2)], sem_s2.at[1])

            @pl.loop(1, 4)
            def _(k):
                both = s_buf.at[1, pl.ds(pair, 2)]
                remote(both, both, sem_send.at[9], sem_s3.at[1], rep=layer * Q + (q + 2 * k) % Q)

    def hand_values():
        @pl.when(w == keeper)
        def _():
            settle(eig_all, sem_e.at[0])

            def hand(t):
                second = jnp.int32(0)
                for e in range(EXTRA):
                    second = jnp.where(t == extra_home(e, core), e, second)
                eig_out[t, 0] = eig_all[owner[r]]
                eig_out[t, 1] = eig_all[owner[LEFT + layer * RIGHT + t]]
                eig_out[t, 2] = eig_all[owner[LEFT + layer * RIGHT + W + second]]

            def send_values(t):
                hand(t)
                remote(eig_out.at[t], eig_in, sem_send.at[14], sem_e.at[1], work=t)

            others(send_values)
            hand(w)
            local(eig_out.at[w], eig_in, sem_e.at[1])

    def pass_on():
        @pl.loop(0, 7)
        def _(k):
            t = partner(w, 0, near_first(k))
            settle(p_share(t), sem_p3.at[t % 8])
            send_across(t)

    tiles_out()
    rows_ready()

    @pl.when(core == 0)
    def _():
        rows_to(1, 0)
        rows_to(1, 1, 7)
        rows_to(1, 2, 6)
        rows_to(1, 3, 5)
        rows_to(1, 4)
        rows_to(0, 1, 7)
        rows_to(0, 2, 6)
        rows_to(0, 3, 5)
        rows_to(0, 4)

    values_out()
    left_tiles()
    extra_tiles_pair()
    right_tiles()
    extra_tiles()
    left_shares()
    right_slabs()
    hand_values()

    @pl.when(core == 1)
    def _():
        rows_to(1, 0)
        rows_to(1, 1, 7)
        rows_to(1, 2, 6)
        rows_to(1, 3, 5)
        rows_to(1, 4)
        rows_to(0, 1, 7)
        rows_to(0, 2, 6)
        rows_to(0, 3, 5)
        rows_to(0, 4)

    pass_on()
    rows_extra(0, 4)
    extra_slabs()

    settle(eig_in, sem_e.at[1])
    left = eig_in[0].astype(F32)
    columns = []
    for c in range(4):
        columns.append(jnp.transpose(jnp.broadcast_to(left[c : c + 1], (128, 128))))
    left_columns = jnp.concatenate(columns, axis=0)

    others_rows = rx.at[0, pl.ds(0, (W - 1) * ROWS), :]
    settle(p_buf.at[:, 0:2], sem_p4)

    def compute(u, j):
        settle(rx.at[u], sem_g.at[u])
        p = p_buf[...].reshape(N, N)
        halves = [slice(c * 256, (c + 1) * 256) for c in range(2)]
        for cols in halves:
            xs[:, cols] = lax.dot_general(
                p, rx[u, :, cols], (((0,), (0,)), ((), ())), preferred_element_type=F32
            ).astype(BF16)
        settle(s_buf.at[u, 0 : 7 - u], sem_s3.at[u])
        s = s_buf[u].reshape(N, N)
        right = eig_in[1 + u].astype(F32)
        for c in range(4):
            cols = slice(c * 128, (c + 1) * 128)
            turned = jnp.dot(xs[...], s[:, cols], preferred_element_type=F32)
            us[:, cols] = (turned / (left_columns * right[c : c + 1] + DAMPING)).astype(BF16)
        for c, cols in enumerate(halves):
            back = lax.dot_general(
                us[...], s[cols], (((1,), (1,)), ((), ())), preferred_element_type=F32
            ).astype(BF16)
            tx[u, c] = jnp.dot(p, back, preferred_element_type=F32).astype(BF16)

            def send_out(t):
                remote(own_rows(t), out_block(t), sem_send.at[10 + u], sem_o, work=t)

            def own_rows(t):
                return tx.at[u, c, pl.ds(pl.multiple_of(t * ROWS, ROWS), ROWS), :]

            def out_block(t):
                return out.at[:, pl.ds(pl.multiple_of(j * N + c * 256, 256), 256)]

            others(send_out)
            local(own_rows(w), out_block(w), sem_o)

    compute(0, w)

    @pl.when(has_extra)
    def _():
        compute(1, W + mine)

    settle(tiles.at[0 : (W - 1) * SLOTS], sem_send.at[0])

    @pl.when(w == keeper)
    def _():
        settle(eig_out.at[0 : W - 1], sem_send.at[14])

    @pl.when(w != keeper)
    def _():
        settle(eig_mine, sem_send.at[1])

    settle(stage_p.at[0 : Q - 1], sem_send.at[4])
    settle(stage_s.at[0 : W - 1], sem_send.at[5])
    settle(rx.at[0, pl.ds(0, 7 * ROWS), :], sem_send.at[7])
    settle(stage_x.at[0], sem_send.at[12])
    settle(p_buf.at[:, 0:2], sem_send.at[13])
    settle(s_buf.at[0, 0:7], sem_send.at[8])
    settle(others_rows, sem_send.at[2])
    settle(others_rows, sem_send.at[10])

    @pl.when(has_extra)
    def _():
        settle(rx.at[0, pl.ds(0, (EXTRA - 1) * ROWS), :], sem_send.at[3])
        settle(stage_s.at[0 : 2 * (EXTRA - 1)], sem_send.at[6])
        settle(s_buf.at[1, 0:6], sem_send.at[9])
        settle(others_rows, sem_send.at[11])

    @pl.when(jnp.logical_not(has_extra))
    def _():
        settle(rx.at[0, pl.ds(0, EXTRA * ROWS), :], sem_send.at[3])
        settle(stage_s.at[0 : 2 * EXTRA], sem_send.at[6])

    settle(out, sem_o)


def per_device(grads, panels, eigvals, owner_slot):
    return pl.pallas_call(
        kernel,
        out_shape=jax.ShapeDtypeStruct(grads.shape, BF16),
        in_specs=[
            pl.BlockSpec(memory_space=pltpu.HBM),
            pl.BlockSpec(memory_space=pltpu.HBM),
            pl.BlockSpec(memory_space=pltpu.HBM),
            pl.BlockSpec(memory_space=pltpu.HBM),
        ],
        out_specs=pl.BlockSpec(memory_space=pl.ANY),
        scratch_shapes=[
            pltpu.SMEM(owner_slot.shape, jnp.int32),
            pltpu.VMEM(grads.shape, BF16),
            pltpu.VMEM((SLOTS, N // Q, N), BF16),
            pltpu.VMEM(eigvals.shape, BF16),
            pltpu.VMEM((W * SLOTS, 16, 128), BF16),
            pltpu.VMEM((W * SLOTS, 16, 128), BF16),
            pltpu.VMEM((SLOTS, 16, 128), BF16),
            pltpu.VMEM((16, 128), F32),
            pltpu.VMEM((W, 3, 16, 128), BF16),
            pltpu.VMEM((3, 16, 128), BF16),
            pltpu.VMEM((W, 16, 128), BF16),
            pltpu.VMEM((2, EXTRA, 16, 128), BF16),
            pltpu.VMEM((Q, 16, 128), BF16),
            pltpu.VMEM((Q, 4, 16, N), BF16),
            pltpu.VMEM((2, Q, 4, 16, N), BF16),
            pltpu.VMEM((2, N, N), BF16),
            pltpu.VMEM((2, 2, N, N // 2), BF16),
            pltpu.VMEM((N, N), BF16),
            pltpu.VMEM((N, N), BF16),
            pltpu.SemaphoreType.DMA((4,)),
            pltpu.SemaphoreType.DMA((15,)),
            pltpu.SemaphoreType.DMA,
            pltpu.SemaphoreType.DMA((2,)),
            pltpu.SemaphoreType.DMA,
            pltpu.SemaphoreType.DMA((8,)),
            pltpu.SemaphoreType.DMA,
            pltpu.SemaphoreType.DMA,
            pltpu.SemaphoreType.DMA((2,)),
            pltpu.SemaphoreType.DMA((2,)),
            pltpu.SemaphoreType.DMA((2,)),
            pltpu.SemaphoreType.DMA,
        ],
        compiler_params=pltpu.CompilerParams(
            collective_id=0, has_side_effects=True, vmem_limit_bytes=32 * 1024 * 1024
        ),
    )(*[pltpu.with_memory_space_constraint(x, pltpu.HBM) for x in (owner_slot, grads, panels, eigvals)])


def solution(mesh):
    return jax.shard_map(
        per_device,
        mesh=mesh,
        in_specs=(P(("rep", "work"), None), P("work", None, None), P("work", None), P()),
        out_specs=P(("rep", "work"), None),
        check_vma=False,
    )
```

```python
import jax
import jax.numpy as jnp
from jax import lax
from jax.experimental import pallas as pl
from jax.experimental.pallas import tpu as pltpu
from jax.sharding import PartitionSpec as P

MESH = pl.DeviceIdType.MESH
N = 512
W = 16
Q = 8
ROWS = 32
RIGHT = 20
LEFT = 16
SLOTS = 4
EXTRA = RIGHT - W
DAMPING = 0.2
BF16 = jnp.bfloat16
F32 = jnp.float32


def partner(w, dx, dz):
    return ((w // 8 + dx) % 2) * 8 + (w % 8 + dz) % 8


def near_first(k):
    return jnp.where(k % 2 == 0, k // 2 + 1, 7 - k // 2)


def extra_home(e, core):
    return (e // 2) * 9 + (e % 2) * 4 + core * 2


def tile(ref, i):
    return ref.at[i // 4, :, pl.ds(pl.multiple_of((i % 4) * 128, 128), 128)]


def kernel(
    owner_hbm, grads_hbm, panels_hbm, eigs_hbm, out,
    owner, grads, panels, eigs,
    tiles, eig_all, eig_mine, eig_f32, eig_slot, eig_out, eig_in,
    stage_s, stage_x, stage_p, p_buf, s_buf, rx, tx, xs, us,
    sem_in, sem_send, sem_t, sem_e, sem_p2, sem_p3, sem_p4, sem_x, sem_s2, sem_s3, sem_g, sem_o,
):
    r = lax.axis_index("rep")
    w = lax.axis_index("work")
    layer = r // Q
    q = r % Q
    core = r % 2
    pair = q - core
    keeper = 2 * q
    extra = jnp.int32(-1)
    for e in range(EXTRA):
        extra = jnp.where(w == extra_home(e, core), e, extra)
    has_extra = extra >= 0
    mine = jnp.where(has_extra, extra, 0)

    barrier = pltpu.get_barrier_semaphore()

    def others_z(body):
        @pl.loop(0, 7)
        def _(k):
            body(partner(w, 0, near_first(k)))

    def others_x(body):
        @pl.loop(0, 7)
        def _(k):
            body(partner(w, 1, near_first(k)))

    def others(body):
        others_z(body)
        body(partner(w, 1, 0))
        others_x(body)

    def mates(body):
        @pl.loop(1, Q)
        def _(k):
            body((q + k) % Q)

    def greet(t):
        pl.semaphore_signal(barrier, inc=1, device_id={"work": t}, device_id_type=MESH)

    def greet_mate(m):
        pl.semaphore_signal(barrier, inc=1, device_id={"rep": layer * Q + m}, device_id_type=MESH)

    others(greet)
    mates(greet_mate)

    def remote(src, dst, send, recv, **where):
        pltpu.make_async_remote_copy(
            src_ref=src, dst_ref=dst, send_sem=send, recv_sem=recv, device_id=where, device_id_type=MESH
        ).start()

    def local(src, dst, sem):
        pltpu.make_async_copy(src, dst, sem).start()

    def settle(ref, sem):
        pltpu.make_async_copy(ref, ref, sem).wait()

    slab = panels_hbm.at[:, pl.ds(pl.multiple_of(q * 64, 64), 64), :]
    local(slab, panels, sem_in.at[0])
    local(eigs_hbm, eigs, sem_in.at[1])
    local(grads_hbm, grads, sem_in.at[2])
    local(owner_hbm, owner, sem_in.at[3])
    settle(panels, sem_in.at[0])
    pl.semaphore_wait(barrier, W - 1 + Q - 1)

    def piece_of(i):
        rows = pl.multiple_of((i // 4) * 16, 16)
        return panels.at[:, pl.ds(rows, 16), pl.ds(pl.multiple_of((i % 4) * 128, 128), 128)]

    def tiles_out():
        def send_tiles(t):
            remote(piece_of(t), tiles.at[pl.ds(w * SLOTS, SLOTS)], sem_send.at[0], sem_t, work=t)

        others(send_tiles)
        local(piece_of(w), tiles.at[pl.ds(w * SLOTS, SLOTS)], sem_t)

    def values_out():
        settle(eigs, sem_in.at[1])

        values = eigs[...].astype(F32)
        for s in range(SLOTS):
            for c in range(4):
                eig_f32[4 * s + c : 4 * s + c + 1, :] = values[s : s + 1, c * 128 : (c + 1) * 128]
        eig_mine[...] = eig_f32[...].astype(BF16)

        @pl.when(w == keeper)
        def _():
            local(eig_mine, eig_all.at[w], sem_e.at[0])

        @pl.when(w != keeper)
        def _():
            remote(eig_mine, eig_all.at[w], sem_send.at[1], sem_e.at[0], work=keeper)

    def block_of(j):
        return grads.at[:, pl.ds(pl.multiple_of(j * N, N), N)]

    def row_slice(ref, u, k):
        return ref.at[u, pl.ds(pl.multiple_of(k * ROWS, ROWS), ROWS), :]

    def send_rows(t):
        remote(block_of(t), row_slice(rx, 0, w), sem_send.at[2], sem_g.at[0], work=t)

    def rows_ready():
        settle(grads, sem_in.at[2])
        rows_own()

    def rows_own():
        local(block_of(w), row_slice(rx, 0, w), sem_g.at[0])

    def rows_to(dx, *steps):
        for dz in steps:
            send_rows(partner(w, dx, dz))

    def rows_extra(a, b):
        @pl.loop(a, b)
        def _(k):
            e = (k + w) % EXTRA
            home = extra_home(e, core)

            @pl.when(home != w)
            def _():
                remote(block_of(W + e), row_slice(rx, 1, w), sem_send.at[3], sem_g.at[1], work=home)

            @pl.when(home == w)
            def _():
                local(block_of(W + e), row_slice(rx, 1, w), sem_g.at[1])

    def p_tile(k):
        return tile(p_buf.at[k], w)

    def left_tiles():
        settle(tiles, sem_t)
        pltpu.make_async_copy(owner_hbm, owner, sem_in.at[3]).wait()

        @pl.loop(0, Q)
        def _(m):
            stage_p[m] = tiles[owner[layer * Q + m]]

        def send_p(m):
            remote(stage_p.at[m], p_tile(q), sem_send.at[4], sem_p2, rep=layer * Q + m)

        mates(send_p)
        local(stage_p.at[q], p_tile(q), sem_p2)

    def extra_tiles_pair():
        @pl.loop(0, EXTRA)
        def _(e):
            stage_x[core, e] = tiles[owner[LEFT + layer * RIGHT + W + e]]

        remote(stage_x.at[core], stage_x.at[core], sem_send.at[12], sem_x, rep=layer * Q + pair + 1 - core)

    def right_tiles():
        @pl.loop(0, W)
        def _(j):
            stage_s[j] = tiles[owner[LEFT + layer * RIGHT + j]]

        def send_s(t):
            remote(stage_s.at[t], tile(s_buf.at[0, q], w), sem_send.at[5], sem_s2.at[0], work=t)

        others(send_s)
        local(stage_s.at[w], tile(s_buf.at[0, q], w), sem_s2.at[0])

    def extra_tiles():
        settle(stage_x.at[0], sem_x)

        def x_tiles():
            return s_buf.at[1, pl.ds(pair, 2), w // 4, :, pl.ds(pl.multiple_of((w % 4) * 128, 128), 128)]

        @pl.loop(0, EXTRA)
        def _(k):
            e = (k + w) % EXTRA
            home = extra_home(e, core)

            @pl.when(home != w)
            def _():
                remote(stage_x.at[:, e], x_tiles(), sem_send.at[6], sem_s2.at[1], work=home)

            @pl.when(home == w)
            def _():
                local(stage_x.at[:, e], x_tiles(), sem_s2.at[1])

    def p_share(k):
        return p_buf.at[:, k // 4, :, pl.ds(pl.multiple_of((k % 4) * 128, 128), 128)]

    def send_across(k):
        remote(p_share(k), p_share(k), sem_send.at[13], sem_p4, work=partner(w, 1, 0))

    def left_shares():
        settle(p_share(w), sem_p2)

        def send_share(t):
            remote(p_share(w), p_share(w), sem_send.at[7], sem_p3.at[w % 8], work=t)

        others_z(send_share)
        send_across(w)

    def right_slabs():
        settle(s_buf.at[0, q], sem_s2.at[0])

        def send_slab(m):
            remote(s_buf.at[0, q], s_buf.at[0, q], sem_send.at[8], sem_s3.at[0], rep=layer * Q + m)

        mates(send_slab)

    def extra_slabs():
        @pl.when(has_extra)
        def _():
            settle(s_buf.at[1, pl.ds(pair, 2)], sem_s2.at[1])

            @pl.loop(1, 4)
            def _(k):
                both = s_buf.at[1, pl.ds(pair, 2)]
                remote(both, both, sem_send.at[9], sem_s3.at[1], rep=layer * Q + (q + 2 * k) % Q)

    def hand_values():
        @pl.when(w == keeper)
        def _():
            settle(eig_all, sem_e.at[0])

            for k in range(W):
                rows = eig_all[k].astype(F32)
                for s in range(SLOTS):
                    eig_slot[k * SLOTS + s, 0:4, :] = rows[4 * s : 4 * s + 4]

            eig_f32[0:4, :] = eig_slot[owner[r], 0:4, :]

            def hand(t):
                second = jnp.int32(0)
                for e in range(EXTRA):
                    second = jnp.where(t == extra_home(e, core), e, second)
                eig_f32[4:8, :] = eig_slot[owner[LEFT + layer * RIGHT + t], 0:4, :]
                eig_f32[8:12, :] = eig_slot[owner[LEFT + layer * RIGHT + W + second], 0:4, :]
                eig_out[t] = eig_f32[...].astype(BF16)

            def send_values(t):
                hand(t)
                remote(eig_out.at[t], eig_in, sem_send.at[14], sem_e.at[1], work=t)

            others(send_values)
            hand(w)
            local(eig_out.at[w], eig_in, sem_e.at[1])

    def pass_on():
        @pl.loop(0, 7)
        def _(k):
            t = partner(w, 0, near_first(k))
            settle(p_share(t), sem_p3.at[t % 8])
            send_across(t)

    tiles_out()
    rows_ready()

    @pl.when(core == 0)
    def _():
        rows_to(1, 0)
        rows_to(1, 1, 7)
        rows_to(1, 2, 6)
        rows_to(1, 3, 5)
        rows_to(1, 4)
        rows_to(0, 1, 7)
        rows_to(0, 2, 6)
        rows_to(0, 3, 5)
        rows_to(0, 4)

    values_out()
    left_tiles()
    extra_tiles_pair()
    right_tiles()
    extra_tiles()
    left_shares()
    hand_values()
    right_slabs()

    @pl.when(core == 1)
    def _():
        rows_to(1, 0)
        rows_to(1, 1, 7)
        rows_to(1, 2, 6)
        rows_to(1, 3, 5)
        rows_to(1, 4)
        rows_to(0, 1, 7)
        rows_to(0, 2, 6)
        rows_to(0, 3, 5)
        rows_to(0, 4)

    pass_on()
    rows_extra(0, 4)
    extra_slabs()

    settle(eig_in, sem_e.at[1])
    values_in = eig_in[...].astype(F32)
    left = values_in[0:4]
    columns = []
    for c in range(4):
        columns.append(jnp.transpose(jnp.broadcast_to(left[c : c + 1], (128, 128))))
    left_columns = jnp.concatenate(columns, axis=0)

    others_rows = rx.at[0, pl.ds(0, (W - 1) * ROWS), :]
    settle(p_buf.at[:, 0:2], sem_p4)

    def compute(u, j):
        settle(rx.at[u], sem_g.at[u])
        p = p_buf[...].reshape(N, N)
        halves = [slice(c * 256, (c + 1) * 256) for c in range(2)]
        for cols in halves:
            xs[:, cols] = lax.dot_general(
                p, rx[u, :, cols], (((0,), (0,)), ((), ())), preferred_element_type=F32
            ).astype(BF16)
        settle(s_buf.at[u, 0 : 7 - u], sem_s3.at[u])
        s = s_buf[u].reshape(N, N)
        right = values_in[4 + 4 * u : 8 + 4 * u]
        for c, cols in enumerate(halves):
            turned = jnp.dot(xs[...], s[:, cols], preferred_element_type=F32)
            outer = [left_columns * right[k : k + 1] for k in (2 * c, 2 * c + 1)]
            us[:, cols] = (turned / (jnp.concatenate(outer, axis=1) + DAMPING)).astype(BF16)
        for c, cols in enumerate(halves):
            back = lax.dot_general(
                us[...], s[cols], (((1,), (1,)), ((), ())), preferred_element_type=F32
            ).astype(BF16)
            tx[u, c] = jnp.dot(p, back, preferred_element_type=F32).astype(BF16)

            def send_out(t):
                remote(own_rows(t), out_block(t), sem_send.at[10 + u], sem_o, work=t)

            def own_rows(t):
                return tx.at[u, c, pl.ds(pl.multiple_of(t * ROWS, ROWS), ROWS), :]

            def out_block(t):
                return out.at[:, pl.ds(pl.multiple_of(j * N + c * 256, 256), 256)]

            others(send_out)
            local(own_rows(w), out_block(w), sem_o)

    compute(0, w)

    @pl.when(has_extra)
    def _():
        compute(1, W + mine)

    settle(tiles.at[0 : (W - 1) * SLOTS], sem_send.at[0])

    @pl.when(w == keeper)
    def _():
        settle(eig_out.at[0 : W - 1], sem_send.at[14])

    @pl.when(w != keeper)
    def _():
        settle(eig_mine, sem_send.at[1])

    settle(stage_p.at[0 : Q - 1], sem_send.at[4])
    settle(stage_s.at[0 : W - 1], sem_send.at[5])
    settle(rx.at[0, pl.ds(0, 7 * ROWS), :], sem_send.at[7])
    settle(stage_x.at[0], sem_send.at[12])
    settle(p_buf.at[:, 0:2], sem_send.at[13])
    settle(s_buf.at[0, 0:7], sem_send.at[8])
    settle(others_rows, sem_send.at[2])
    settle(others_rows, sem_send.at[10])

    @pl.when(has_extra)
    def _():
        settle(rx.at[0, pl.ds(0, (EXTRA - 1) * ROWS), :], sem_send.at[3])
        settle(stage_s.at[0 : 2 * (EXTRA - 1)], sem_send.at[6])
        settle(s_buf.at[1, 0:6], sem_send.at[9])
        settle(others_rows, sem_send.at[11])

    @pl.when(jnp.logical_not(has_extra))
    def _():
        settle(rx.at[0, pl.ds(0, EXTRA * ROWS), :], sem_send.at[3])
        settle(stage_s.at[0 : 2 * EXTRA], sem_send.at[6])

    settle(out, sem_o)


def per_device(grads, panels, eigvals, owner_slot):
    return pl.pallas_call(
        kernel,
        out_shape=jax.ShapeDtypeStruct(grads.shape, BF16),
        in_specs=[
            pl.BlockSpec(memory_space=pltpu.HBM),
            pl.BlockSpec(memory_space=pltpu.HBM),
            pl.BlockSpec(memory_space=pltpu.HBM),
            pl.BlockSpec(memory_space=pltpu.HBM),
        ],
        out_specs=pl.BlockSpec(memory_space=pl.ANY),
        scratch_shapes=[
            pltpu.SMEM(owner_slot.shape, jnp.int32),
            pltpu.VMEM(grads.shape, BF16),
            pltpu.VMEM((SLOTS, N // Q, N), BF16),
            pltpu.VMEM(eigvals.shape, BF16),
            pltpu.VMEM((W * SLOTS, 16, 128), BF16),
            pltpu.VMEM((W, 16, 128), BF16),
            pltpu.VMEM((16, 128), BF16),
            pltpu.VMEM((16, 128), F32),
            pltpu.VMEM((W * SLOTS, 8, 128), F32),
            pltpu.VMEM((W, 16, 128), BF16),
            pltpu.VMEM((16, 128), BF16),
            pltpu.VMEM((W, 16, 128), BF16),
            pltpu.VMEM((2, EXTRA, 16, 128), BF16),
            pltpu.VMEM((Q, 16, 128), BF16),
            pltpu.VMEM((Q, 4, 16, N), BF16),
            pltpu.VMEM((2, Q, 4, 16, N), BF16),
            pltpu.VMEM((2, N, N), BF16),
            pltpu.VMEM((2, 2, N, N // 2), BF16),
            pltpu.VMEM((N, N), BF16),
            pltpu.VMEM((N, N), BF16),
            pltpu.SemaphoreType.DMA((4,)),
            pltpu.SemaphoreType.DMA((15,)),
            pltpu.SemaphoreType.DMA,
            pltpu.SemaphoreType.DMA((2,)),
            pltpu.SemaphoreType.DMA,
            pltpu.SemaphoreType.DMA((8,)),
            pltpu.SemaphoreType.DMA,
            pltpu.SemaphoreType.DMA,
            pltpu.SemaphoreType.DMA((2,)),
            pltpu.SemaphoreType.DMA((2,)),
            pltpu.SemaphoreType.DMA((2,)),
            pltpu.SemaphoreType.DMA,
        ],
        compiler_params=pltpu.CompilerParams(
            collective_id=0, has_side_effects=True, vmem_limit_bytes=32 * 1024 * 1024
        ),
    )(*[pltpu.with_memory_space_constraint(x, pltpu.HBM) for x in (owner_slot, grads, panels, eigvals)])


def solution(mesh):
    return jax.shard_map(
        per_device,
        mesh=mesh,
        in_specs=(P(("rep", "work"), None), P("work", None, None), P("work", None), P()),
        out_specs=P(("rep", "work"), None),
        check_vma=False,
    )
```

```python
import jax
import jax.numpy as jnp
from jax import lax
from jax.experimental import pallas as pl
from jax.experimental.pallas import tpu as pltpu
from jax.sharding import PartitionSpec as P

MESH = pl.DeviceIdType.MESH
N = 512
W = 16
Q = 8
ROWS = 32
RIGHT = 20
LEFT = 16
SLOTS = 4
EXTRA = RIGHT - W
DAMPING = 0.2
BF16 = jnp.bfloat16
F32 = jnp.float32


def partner(w, dx, dz):
    return ((w // 8 + dx) % 2) * 8 + (w % 8 + dz) % 8


def near_first(k):
    return jnp.where(k % 2 == 0, k // 2 + 1, 7 - k // 2)


def extra_home(e, core):
    return (e // 2) * 9 + (e % 2) * 4 + core * 2


def tile(ref, i):
    return ref.at[i // 4, :, pl.ds(pl.multiple_of((i % 4) * 128, 128), 128)]


def kernel(
    owner_hbm, grads_hbm, panels_hbm, eigs_hbm, out,
    owner, grads, panels, eigs,
    tiles, eig_all, eig_mine, eig_f32, eig_slot, eig_out, eig_in,
    stage_s, stage_x, stage_p, p_buf, s_buf, rx, tx, xs, us,
    sem_in, sem_send, sem_t, sem_e, sem_p2, sem_p3, sem_p4, sem_x, sem_s2, sem_s3, sem_g, sem_o,
):
    r = lax.axis_index("rep")
    w = lax.axis_index("work")
    layer = r // Q
    q = r % Q
    core = r % 2
    pair = q - core
    keeper = 2 * q
    extra = jnp.int32(-1)
    for e in range(EXTRA):
        extra = jnp.where(w == extra_home(e, core), e, extra)
    has_extra = extra >= 0
    mine = jnp.where(has_extra, extra, 0)

    barrier = pltpu.get_barrier_semaphore()

    def others_z(body):
        @pl.loop(0, 7)
        def _(k):
            body(partner(w, 0, near_first(k)))

    def others_x(body):
        @pl.loop(0, 7)
        def _(k):
            body(partner(w, 1, near_first(k)))

    def others(body):
        others_z(body)
        body(partner(w, 1, 0))
        others_x(body)

    def mates(body):
        @pl.loop(1, Q)
        def _(k):
            body((q + k) % Q)

    def greet(t):
        pl.semaphore_signal(barrier, inc=1, device_id={"work": t}, device_id_type=MESH)

    def greet_mate(m):
        pl.semaphore_signal(barrier, inc=1, device_id={"rep": layer * Q + m}, device_id_type=MESH)

    for dz in (4, 3, 5, 2, 6, 1, 7, 0):
        greet(partner(w, 1, dz))
        if dz:
            greet(partner(w, 0, dz))
    mates(greet_mate)

    def remote(src, dst, send, recv, **where):
        pltpu.make_async_remote_copy(
            src_ref=src, dst_ref=dst, send_sem=send, recv_sem=recv, device_id=where, device_id_type=MESH
        ).start()

    def local(src, dst, sem):
        pltpu.make_async_copy(src, dst, sem).start()

    def settle(ref, sem):
        pltpu.make_async_copy(ref, ref, sem).wait()

    slab = panels_hbm.at[:, pl.ds(pl.multiple_of(q * 64, 64), 64), :]
    local(slab, panels, sem_in.at[0])
    local(eigs_hbm, eigs, sem_in.at[1])
    local(grads_hbm, grads, sem_in.at[2])
    local(owner_hbm, owner, sem_in.at[3])
    settle(panels, sem_in.at[0])
    pl.semaphore_wait(barrier, W - 1 + Q - 1)

    def piece_of(i):
        rows = pl.multiple_of((i // 4) * 16, 16)
        return panels.at[:, pl.ds(rows, 16), pl.ds(pl.multiple_of((i % 4) * 128, 128), 128)]

    def tiles_out():
        def send_tiles(t):
            remote(piece_of(t), tiles.at[pl.ds(w * SLOTS, SLOTS)], sem_send.at[0], sem_t, work=t)

        for dz in (1, 7, 2, 6, 3, 5, 4):
            send_tiles(partner(w, 0, dz))
        send_tiles(partner(w, 1, 0))
        for dz in (4, 3, 5, 2, 6, 1, 7):
            send_tiles(partner(w, 1, dz))
        local(piece_of(w), tiles.at[pl.ds(w * SLOTS, SLOTS)], sem_t)

    def values_out():
        settle(eigs, sem_in.at[1])

        values = eigs[...].astype(F32)
        for s in range(SLOTS):
            for c in range(4):
                eig_f32[4 * s + c : 4 * s + c + 1, :] = values[s : s + 1, c * 128 : (c + 1) * 128]
        eig_mine[...] = eig_f32[...].astype(BF16)

        @pl.when(w == keeper)
        def _():
            local(eig_mine, eig_all.at[w], sem_e.at[0])

        @pl.when(w != keeper)
        def _():
            remote(eig_mine, eig_all.at[w], sem_send.at[1], sem_e.at[0], work=keeper)

    def block_of(j):
        return grads.at[:, pl.ds(pl.multiple_of(j * N, N), N)]

    def row_slice(ref, u, k):
        return ref.at[u, pl.ds(pl.multiple_of(k * ROWS, ROWS), ROWS), :]

    def send_rows(t):
        remote(block_of(t), row_slice(rx, 0, w), sem_send.at[2], sem_g.at[0], work=t)

    def rows_ready():
        settle(grads, sem_in.at[2])
        rows_own()

    def rows_own():
        local(block_of(w), row_slice(rx, 0, w), sem_g.at[0])

    def rows_to(dx, *steps):
        for dz in steps:
            send_rows(partner(w, dx, dz))

    def rows_extra(a, b):
        @pl.loop(a, b)
        def _(k):
            e = (k + w) % EXTRA
            home = extra_home(e, core)

            @pl.when(home != w)
            def _():
                remote(block_of(W + e), row_slice(rx, 1, w), sem_send.at[3], sem_g.at[1], work=home)

            @pl.when(home == w)
            def _():
                local(block_of(W + e), row_slice(rx, 1, w), sem_g.at[1])

    def p_tile(k):
        return tile(p_buf.at[k], w)

    def left_tiles():
        settle(tiles, sem_t)
        pltpu.make_async_copy(owner_hbm, owner, sem_in.at[3]).wait()

        @pl.loop(0, Q)
        def _(m):
            stage_p[m] = tiles[owner[layer * Q + m]]

        def send_p(m):
            remote(stage_p.at[m], p_tile(q), sem_send.at[4], sem_p2, rep=layer * Q + m)

        mates(send_p)
        local(stage_p.at[q], p_tile(q), sem_p2)

    def extra_tiles_pair():
        @pl.loop(0, EXTRA)
        def _(e):
            stage_x[core, e] = tiles[owner[LEFT + layer * RIGHT + W + e]]

        remote(stage_x.at[core], stage_x.at[core], sem_send.at[12], sem_x, rep=layer * Q + pair + 1 - core)

    def right_tiles():
        @pl.loop(0, W)
        def _(j):
            stage_s[j] = tiles[owner[LEFT + layer * RIGHT + j]]

        def send_s(t):
            remote(stage_s.at[t], tile(s_buf.at[0, q], w), sem_send.at[5], sem_s2.at[0], work=t)

        others(send_s)
        local(stage_s.at[w], tile(s_buf.at[0, q], w), sem_s2.at[0])

    def extra_tiles():
        settle(stage_x.at[0], sem_x)

        def x_tiles():
            return s_buf.at[1, pl.ds(pair, 2), w // 4, :, pl.ds(pl.multiple_of((w % 4) * 128, 128), 128)]

        @pl.loop(0, EXTRA)
        def _(k):
            e = (k + w) % EXTRA
            home = extra_home(e, core)

            @pl.when(home != w)
            def _():
                remote(stage_x.at[:, e], x_tiles(), sem_send.at[6], sem_s2.at[1], work=home)

            @pl.when(home == w)
            def _():
                local(stage_x.at[:, e], x_tiles(), sem_s2.at[1])

    def p_share(k):
        return p_buf.at[:, k // 4, :, pl.ds(pl.multiple_of((k % 4) * 128, 128), 128)]

    def send_across(k):
        remote(p_share(k), p_share(k), sem_send.at[13], sem_p4, work=partner(w, 1, 0))

    def left_shares():
        settle(p_share(w), sem_p2)

        def send_share(t):
            remote(p_share(w), p_share(w), sem_send.at[7], sem_p3.at[w % 8], work=t)

        others_z(send_share)
        send_across(w)

    def right_slabs():
        settle(s_buf.at[0, q], sem_s2.at[0])

        def send_slab(m):
            remote(s_buf.at[0, q], s_buf.at[0, q], sem_send.at[8], sem_s3.at[0], rep=layer * Q + m)

        mates(send_slab)

    def extra_slabs():
        @pl.when(has_extra)
        def _():
            settle(s_buf.at[1, pl.ds(pair, 2)], sem_s2.at[1])

            @pl.loop(1, 4)
            def _(k):
                both = s_buf.at[1, pl.ds(pair, 2)]
                remote(both, both, sem_send.at[9], sem_s3.at[1], rep=layer * Q + (q + 2 * k) % Q)

    def hand_values():
        @pl.when(w == keeper)
        def _():
            settle(eig_all, sem_e.at[0])

            for k in range(W):
                rows = eig_all[k].astype(F32)
                for s in range(SLOTS):
                    eig_slot[k * SLOTS + s, 0:4, :] = rows[4 * s : 4 * s + 4]

            eig_f32[0:4, :] = eig_slot[owner[r], 0:4, :]

            def hand(t):
                second = jnp.int32(0)
                for e in range(EXTRA):
                    second = jnp.where(t == extra_home(e, core), e, second)
                eig_f32[4:8, :] = eig_slot[owner[LEFT + layer * RIGHT + t], 0:4, :]
                eig_f32[8:12, :] = eig_slot[owner[LEFT + layer * RIGHT + W + second], 0:4, :]
                eig_out[t] = eig_f32[...].astype(BF16)

            def send_values(t):
                hand(t)
                remote(eig_out.at[t], eig_in, sem_send.at[14], sem_e.at[1], work=t)

            others(send_values)
            hand(w)
            local(eig_out.at[w], eig_in, sem_e.at[1])

    def pass_on():
        @pl.loop(0, 7)
        def _(k):
            t = partner(w, 0, near_first(k))
            settle(p_share(t), sem_p3.at[t % 8])
            send_across(t)

    tiles_out()
    rows_ready()

    @pl.when(core == 0)
    def _():
        rows_to(1, 0)
        rows_to(1, 1, 7)
        rows_to(1, 2, 6)
        rows_to(1, 3, 5)
        rows_to(1, 4)
        rows_to(0, 1, 7)
        rows_to(0, 2, 6)
        rows_to(0, 3, 5)
        rows_to(0, 4)

    values_out()
    left_tiles()
    extra_tiles_pair()
    right_tiles()
    extra_tiles()
    left_shares()
    hand_values()
    right_slabs()

    @pl.when(core == 1)
    def _():
        rows_to(1, 0)
        rows_to(1, 1, 7)
        rows_to(1, 2, 6)
        rows_to(1, 3, 5)
        rows_to(1, 4)
        rows_to(0, 1, 7)
        rows_to(0, 2, 6)
        rows_to(0, 3, 5)
        rows_to(0, 4)

    pass_on()
    extra_slabs()
    rows_extra(0, 4)

    settle(eig_in, sem_e.at[1])
    values_in = eig_in[...].astype(F32)
    left = values_in[0:4]
    columns = []
    for c in range(4):
        columns.append(jnp.transpose(jnp.broadcast_to(left[c : c + 1], (128, 128))))
    left_columns = jnp.concatenate(columns, axis=0)

    others_rows = rx.at[0, pl.ds(0, (W - 1) * ROWS), :]
    settle(p_buf.at[:, 0:2], sem_p4)

    def compute(u, j):
        settle(rx.at[u], sem_g.at[u])
        p = p_buf[...].reshape(N, N)
        halves = [slice(c * 256, (c + 1) * 256) for c in range(2)]
        for cols in halves:
            xs[:, cols] = lax.dot_general(
                p, rx[u, :, cols], (((0,), (0,)), ((), ())), preferred_element_type=F32
            ).astype(BF16)
        settle(s_buf.at[u, 0 : 7 - u], sem_s3.at[u])
        s = s_buf[u].reshape(N, N)
        right = values_in[4 + 4 * u : 8 + 4 * u]
        for c, cols in enumerate(halves):
            turned = jnp.dot(xs[...], s[:, cols], preferred_element_type=F32)
            outer = [left_columns * right[k : k + 1] for k in (2 * c, 2 * c + 1)]
            us[:, cols] = (turned / (jnp.concatenate(outer, axis=1) + DAMPING)).astype(BF16)
        for c, cols in enumerate(halves):
            xs[:, cols] = lax.dot_general(
                us[...], s[cols], (((1,), (1,)), ((), ())), preferred_element_type=F32
            ).astype(BF16)
            tx[u, c] = jnp.dot(p, xs[:, cols], preferred_element_type=F32).astype(BF16)

            def send_out(t):
                remote(own_rows(t), out_block(t), sem_send.at[10 + u], sem_o, work=t)

            def own_rows(t):
                return tx.at[u, c, pl.ds(pl.multiple_of(t * ROWS, ROWS), ROWS), :]

            def out_block(t):
                return out.at[:, pl.ds(pl.multiple_of(j * N + c * 256, 256), 256)]

            others(send_out)
            local(own_rows(w), out_block(w), sem_o)

    compute(0, w)

    @pl.when(has_extra)
    def _():
        compute(1, W + mine)

    settle(tiles.at[0 : (W - 1) * SLOTS], sem_send.at[0])

    @pl.when(w == keeper)
    def _():
        settle(eig_out.at[0 : W - 1], sem_send.at[14])

    @pl.when(w != keeper)
    def _():
        settle(eig_mine, sem_send.at[1])

    settle(stage_p.at[0 : Q - 1], sem_send.at[4])
    settle(stage_s.at[0 : W - 1], sem_send.at[5])
    settle(rx.at[0, pl.ds(0, 7 * ROWS), :], sem_send.at[7])
    settle(stage_x.at[0], sem_send.at[12])
    settle(p_buf.at[:, 0:2], sem_send.at[13])
    settle(s_buf.at[0, 0:7], sem_send.at[8])
    settle(others_rows, sem_send.at[2])
    settle(others_rows, sem_send.at[10])

    @pl.when(has_extra)
    def _():
        settle(rx.at[0, pl.ds(0, (EXTRA - 1) * ROWS), :], sem_send.at[3])
        settle(stage_s.at[0 : 2 * (EXTRA - 1)], sem_send.at[6])
        settle(s_buf.at[1, 0:6], sem_send.at[9])
        settle(others_rows, sem_send.at[11])

    @pl.when(jnp.logical_not(has_extra))
    def _():
        settle(rx.at[0, pl.ds(0, EXTRA * ROWS), :], sem_send.at[3])
        settle(stage_s.at[0 : 2 * EXTRA], sem_send.at[6])

    settle(out, sem_o)


def per_device(grads, panels, eigvals, owner_slot):
    return pl.pallas_call(
        kernel,
        out_shape=jax.ShapeDtypeStruct(grads.shape, BF16),
        in_specs=[
            pl.BlockSpec(memory_space=pltpu.HBM),
            pl.BlockSpec(memory_space=pltpu.HBM),
            pl.BlockSpec(memory_space=pltpu.HBM),
            pl.BlockSpec(memory_space=pltpu.HBM),
        ],
        out_specs=pl.BlockSpec(memory_space=pl.ANY),
        scratch_shapes=[
            pltpu.SMEM(owner_slot.shape, jnp.int32),
            pltpu.VMEM(grads.shape, BF16),
            pltpu.VMEM((SLOTS, N // Q, N), BF16),
            pltpu.VMEM(eigvals.shape, BF16),
            pltpu.VMEM((W * SLOTS, 16, 128), BF16),
            pltpu.VMEM((W, 16, 128), BF16),
            pltpu.VMEM((16, 128), BF16),
            pltpu.VMEM((16, 128), F32),
            pltpu.VMEM((W * SLOTS, 8, 128), F32),
            pltpu.VMEM((W, 16, 128), BF16),
            pltpu.VMEM((16, 128), BF16),
            pltpu.VMEM((W, 16, 128), BF16),
            pltpu.VMEM((2, EXTRA, 16, 128), BF16),
            pltpu.VMEM((Q, 16, 128), BF16),
            pltpu.VMEM((Q, 4, 16, N), BF16),
            pltpu.VMEM((2, Q, 4, 16, N), BF16),
            pltpu.VMEM((2, N, N), BF16),
            pltpu.VMEM((2, 2, N, N // 2), BF16),
            pltpu.VMEM((N, N), BF16),
            pltpu.VMEM((N, N), BF16),
            pltpu.SemaphoreType.DMA((4,)),
            pltpu.SemaphoreType.DMA((15,)),
            pltpu.SemaphoreType.DMA,
            pltpu.SemaphoreType.DMA((2,)),
            pltpu.SemaphoreType.DMA,
            pltpu.SemaphoreType.DMA((8,)),
            pltpu.SemaphoreType.DMA,
            pltpu.SemaphoreType.DMA,
            pltpu.SemaphoreType.DMA((2,)),
            pltpu.SemaphoreType.DMA((2,)),
            pltpu.SemaphoreType.DMA((2,)),
            pltpu.SemaphoreType.DMA,
        ],
        compiler_params=pltpu.CompilerParams(
            collective_id=0, has_side_effects=True, vmem_limit_bytes=32 * 1024 * 1024
        ),
    )(*[pltpu.with_memory_space_constraint(x, pltpu.HBM) for x in (owner_slot, grads, panels, eigvals)])


def solution(mesh):
    return jax.shard_map(
        per_device,
        mesh=mesh,
        in_specs=(P(("rep", "work"), None), P("work", None, None), P("work", None), P()),
        out_specs=P(("rep", "work"), None),
        check_vma=False,
    )
```

```python
import jax
import jax.numpy as jnp
from jax import lax
from jax.experimental import pallas as pl
from jax.experimental.pallas import tpu as pltpu
from jax.sharding import PartitionSpec as P

MESH = pl.DeviceIdType.MESH
N = 512
W = 16
Q = 8
ROWS = 32
RIGHT = 20
LEFT = 16
SLOTS = 4
EXTRA = RIGHT - W
DAMPING = 0.2
BF16 = jnp.bfloat16
F32 = jnp.float32


def partner(w, dx, dz):
    return ((w // 8 + dx) % 2) * 8 + (w % 8 + dz) % 8


def near_first(k):
    return jnp.where(k % 2 == 0, k // 2 + 1, 7 - k // 2)


def extra_home(e, core):
    return (e // 2) * 9 + (e % 2) * 4 + core * 2


def tile(ref, i):
    return ref.at[i // 4, :, pl.ds(pl.multiple_of((i % 4) * 128, 128), 128)]


def kernel(
    owner_hbm, grads_hbm, panels_hbm, eigs_hbm, out,
    owner, grads, panels, eigs,
    tiles, eig_all, eig_mine, eig_f32, eig_slot, eig_out, eig_in,
    stage_s, stage_x, stage_p, p_buf, s_buf, rx, tx, xs, us,
    sem_in, sem_send, sem_t, sem_e, sem_p2, sem_p3, sem_p4, sem_x, sem_s2, sem_s3, sem_g, sem_o,
):
    r = lax.axis_index("rep")
    w = lax.axis_index("work")
    layer = r // Q
    q = r % Q
    core = r % 2
    pair = q - core
    keeper = 2 * q
    extra = jnp.int32(-1)
    for e in range(EXTRA):
        extra = jnp.where(w == extra_home(e, core), e, extra)
    has_extra = extra >= 0
    mine = jnp.where(has_extra, extra, 0)

    barrier = pltpu.get_barrier_semaphore()

    def others_z(body):
        @pl.loop(0, 7)
        def _(k):
            body(partner(w, 0, near_first(k)))

    def others_x(body):
        @pl.loop(0, 7)
        def _(k):
            body(partner(w, 1, near_first(k)))

    def others(body):
        others_z(body)
        body(partner(w, 1, 0))
        others_x(body)

    def mates(body):
        @pl.loop(1, Q)
        def _(k):
            body((q + k) % Q)

    def greet(t):
        pl.semaphore_signal(barrier, inc=1, device_id={"work": t}, device_id_type=MESH)

    def greet_mate(m):
        pl.semaphore_signal(barrier, inc=1, device_id={"rep": layer * Q + m}, device_id_type=MESH)

    for dz in (4, 3, 5, 2, 6, 1, 7, 0):
        greet(partner(w, 1, dz))
        if dz:
            greet(partner(w, 0, dz))
    mates(greet_mate)

    def remote(src, dst, send, recv, **where):
        pltpu.make_async_remote_copy(
            src_ref=src, dst_ref=dst, send_sem=send, recv_sem=recv, device_id=where, device_id_type=MESH
        ).start()

    def local(src, dst, sem):
        pltpu.make_async_copy(src, dst, sem).start()

    def settle(ref, sem):
        pltpu.make_async_copy(ref, ref, sem).wait()

    slab = panels_hbm.at[:, pl.ds(pl.multiple_of(q * 64, 64), 64), :]
    local(slab, panels, sem_in.at[0])
    local(eigs_hbm, eigs, sem_in.at[1])
    local(grads_hbm, grads, sem_in.at[2])
    local(owner_hbm, owner, sem_in.at[3])
    settle(panels, sem_in.at[0])
    pl.semaphore_wait(barrier, W - 1 + Q - 1)

    def piece_of(i):
        rows = pl.multiple_of((i // 4) * 16, 16)
        return panels.at[:, pl.ds(rows, 16), pl.ds(pl.multiple_of((i % 4) * 128, 128), 128)]

    def tiles_out():
        def send_tiles(t):
            remote(piece_of(t), tiles.at[pl.ds(w * SLOTS, SLOTS)], sem_send.at[0], sem_t, work=t)

        for dz in (1, 7, 2, 6, 3, 5, 4):
            send_tiles(partner(w, 0, dz))
        send_tiles(partner(w, 1, 0))
        for dz in (4, 3, 5, 2, 6, 1, 7):
            send_tiles(partner(w, 1, dz))
        local(piece_of(w), tiles.at[pl.ds(w * SLOTS, SLOTS)], sem_t)

    def values_out():
        settle(eigs, sem_in.at[1])

        values = eigs[...].astype(F32)
        for s in range(SLOTS):
            for c in range(4):
                eig_f32[4 * s + c : 4 * s + c + 1, :] = values[s : s + 1, c * 128 : (c + 1) * 128]
        eig_mine[...] = eig_f32[...].astype(BF16)

        @pl.when(w == keeper)
        def _():
            local(eig_mine, eig_all.at[w], sem_e.at[0])

        @pl.when(w != keeper)
        def _():
            remote(eig_mine, eig_all.at[w], sem_send.at[1], sem_e.at[0], work=keeper)

    def block_of(j):
        return grads.at[:, pl.ds(pl.multiple_of(j * N, N), N)]

    def row_slice(ref, u, k):
        return ref.at[u, pl.ds(pl.multiple_of(k * ROWS, ROWS), ROWS), :]

    def send_rows(t):
        remote(block_of(t), row_slice(rx, 0, w), sem_send.at[2], sem_g.at[0], work=t)

    def rows_ready():
        settle(grads, sem_in.at[2])
        rows_own()

    def rows_own():
        local(block_of(w), row_slice(rx, 0, w), sem_g.at[0])

    def rows_to(dx, *steps):
        for dz in steps:
            send_rows(partner(w, dx, dz))

    def rows_extra(a, b):
        @pl.loop(a, b)
        def _(k):
            e = (k + w) % EXTRA
            home = extra_home(e, core)

            @pl.when(home != w)
            def _():
                remote(block_of(W + e), row_slice(rx, 1, w), sem_send.at[3], sem_g.at[1], work=home)

            @pl.when(home == w)
            def _():
                local(block_of(W + e), row_slice(rx, 1, w), sem_g.at[1])

    def p_tile(k):
        return tile(p_buf.at[k], w)

    def left_tiles():
        settle(tiles, sem_t)
        pltpu.make_async_copy(owner_hbm, owner, sem_in.at[3]).wait()

        @pl.loop(0, Q)
        def _(m):
            stage_p[m] = tiles[owner[layer * Q + m]]

        def send_p(m):
            remote(stage_p.at[m], p_tile(q), sem_send.at[4], sem_p2, rep=layer * Q + m)

        mates(send_p)
        local(stage_p.at[q], p_tile(q), sem_p2)

    def extra_tiles_pair():
        @pl.loop(0, EXTRA)
        def _(e):
            stage_x[core, e] = tiles[owner[LEFT + layer * RIGHT + W + e]]

        remote(stage_x.at[core], stage_x.at[core], sem_send.at[12], sem_x, rep=layer * Q + pair + 1 - core)

    def right_tiles():
        @pl.loop(0, W)
        def _(j):
            stage_s[j] = tiles[owner[LEFT + layer * RIGHT + j]]

        def send_s(t):
            remote(stage_s.at[t], tile(s_buf.at[0, q], w), sem_send.at[5], sem_s2.at[0], work=t)

        others_z(send_s)
        send_s(partner(w, 1, 0))
        for dz in (4, 3, 5, 2, 6, 1, 7):
            send_s(partner(w, 1, dz))
        local(stage_s.at[w], tile(s_buf.at[0, q], w), sem_s2.at[0])

    def extra_tiles():
        settle(stage_x.at[0], sem_x)

        def x_tiles():
            return s_buf.at[1, pl.ds(pair, 2), w // 4, :, pl.ds(pl.multiple_of((w % 4) * 128, 128), 128)]

        @pl.loop(0, EXTRA)
        def _(k):
            e = (k + w) % EXTRA
            home = extra_home(e, core)

            @pl.when(home != w)
            def _():
                remote(stage_x.at[:, e], x_tiles(), sem_send.at[6], sem_s2.at[1], work=home)

            @pl.when(home == w)
            def _():
                local(stage_x.at[:, e], x_tiles(), sem_s2.at[1])

    def p_share(k):
        return p_buf.at[:, k // 4, :, pl.ds(pl.multiple_of((k % 4) * 128, 128), 128)]

    def send_across(k):
        remote(p_share(k), p_share(k), sem_send.at[13], sem_p4, work=partner(w, 1, 0))

    def left_shares():
        settle(p_share(w), sem_p2)

        def send_share(t):
            remote(p_share(w), p_share(w), sem_send.at[7], sem_p3.at[w % 8], work=t)

        others_z(send_share)
        send_across(w)

    def right_slabs():
        settle(s_buf.at[0, q], sem_s2.at[0])

        def send_slab(m):
            remote(s_buf.at[0, q], s_buf.at[0, q], sem_send.at[8], sem_s3.at[0], rep=layer * Q + m)

        mates(send_slab)

    def extra_slabs():
        @pl.when(has_extra)
        def _():
            settle(s_buf.at[1, pl.ds(pair, 2)], sem_s2.at[1])

            @pl.loop(1, 4)
            def _(k):
                both = s_buf.at[1, pl.ds(pair, 2)]
                remote(both, both, sem_send.at[9], sem_s3.at[1], rep=layer * Q + (q + 2 * k) % Q)

    def hand_values():
        @pl.when(w == keeper)
        def _():
            settle(eig_all, sem_e.at[0])

            for k in range(W):
                rows = eig_all[k].astype(F32)
                for s in range(SLOTS):
                    eig_slot[k * SLOTS + s, 0:4, :] = rows[4 * s : 4 * s + 4]

            eig_f32[0:4, :] = eig_slot[owner[r], 0:4, :]

            def hand(t):
                second = jnp.int32(0)
                for e in range(EXTRA):
                    second = jnp.where(t == extra_home(e, core), e, second)
                eig_f32[4:8, :] = eig_slot[owner[LEFT + layer * RIGHT + t], 0:4, :]
                eig_f32[8:12, :] = eig_slot[owner[LEFT + layer * RIGHT + W + second], 0:4, :]
                eig_out[t] = eig_f32[...].astype(BF16)

            def send_values(t):
                hand(t)
                remote(eig_out.at[t], eig_in, sem_send.at[14], sem_e.at[1], work=t)

            others(send_values)
            hand(w)
            local(eig_out.at[w], eig_in, sem_e.at[1])

    def pass_on():
        @pl.loop(0, 7)
        def _(k):
            t = partner(w, 0, near_first(k))
            settle(p_share(t), sem_p3.at[t % 8])
            send_across(t)

    tiles_out()
    rows_ready()

    @pl.when(core == 0)
    def _():
        rows_to(1, 0)
        rows_to(1, 1, 7)
        rows_to(1, 2, 6)
        rows_to(1, 3, 5)
        rows_to(1, 4)
        rows_to(0, 1, 7)
        rows_to(0, 2, 6)
        rows_to(0, 3, 5)
        rows_to(0, 4)

    values_out()
    left_tiles()
    extra_tiles_pair()
    right_tiles()
    extra_tiles()
    left_shares()
    hand_values()
    right_slabs()

    @pl.when(core == 1)
    def _():
        rows_to(1, 0)
        rows_to(1, 1, 7)
        rows_to(1, 2, 6)
        rows_to(1, 3, 5)
        rows_to(1, 4)
        rows_to(0, 1, 7)
        rows_to(0, 2, 6)
        rows_to(0, 3, 5)
        rows_to(0, 4)

    pass_on()
    extra_slabs()
    rows_extra(0, 4)

    settle(eig_in, sem_e.at[1])
    values_in = eig_in[...].astype(F32)
    left = values_in[0:4]
    columns = []
    for c in range(4):
        columns.append(jnp.transpose(jnp.broadcast_to(left[c : c + 1], (128, 128))))
    left_columns = jnp.concatenate(columns, axis=0)

    others_rows = rx.at[0, pl.ds(0, (W - 1) * ROWS), :]
    settle(p_buf.at[:, 0:2], sem_p4)

    def compute(u, j):
        settle(rx.at[u], sem_g.at[u])
        p = p_buf[...].reshape(N, N)
        halves = [slice(c * 256, (c + 1) * 256) for c in range(2)]
        for cols in halves:
            xs[:, cols] = lax.dot_general(
                p, rx[u, :, cols], (((0,), (0,)), ((), ())), preferred_element_type=F32
            ).astype(BF16)
        settle(s_buf.at[u, 0 : 7 - u], sem_s3.at[u])
        s = s_buf[u].reshape(N, N)
        right = values_in[4 + 4 * u : 8 + 4 * u]
        for c, cols in enumerate(halves):
            turned = jnp.dot(xs[...], s[:, cols], preferred_element_type=F32)
            outer = [left_columns * right[k : k + 1] for k in (2 * c, 2 * c + 1)]
            us[:, cols] = (turned / (jnp.concatenate(outer, axis=1) + DAMPING)).astype(BF16)
        for c, cols in enumerate(halves):
            xs[:, cols] = lax.dot_general(
                us[...], s[cols], (((1,), (1,)), ((), ())), preferred_element_type=F32
            ).astype(BF16)
            tx[u, c] = jnp.dot(p, xs[:, cols], preferred_element_type=F32).astype(BF16)

            def send_out(t):
                remote(own_rows(t), out_block(t), sem_send.at[10 + u], sem_o, work=t)

            def own_rows(t):
                return tx.at[u, c, pl.ds(pl.multiple_of(t * ROWS, ROWS), ROWS), :]

            def out_block(t):
                return out.at[:, pl.ds(pl.multiple_of(j * N + c * 256, 256), 256)]

            others(send_out)
            local(own_rows(w), out_block(w), sem_o)

    compute(0, w)

    @pl.when(has_extra)
    def _():
        compute(1, W + mine)

    settle(tiles.at[0 : (W - 1) * SLOTS], sem_send.at[0])

    @pl.when(w == keeper)
    def _():
        settle(eig_out.at[0 : W - 1], sem_send.at[14])

    @pl.when(w != keeper)
    def _():
        settle(eig_mine, sem_send.at[1])

    settle(stage_p.at[0 : Q - 1], sem_send.at[4])
    settle(stage_s.at[0 : W - 1], sem_send.at[5])
    settle(rx.at[0, pl.ds(0, 7 * ROWS), :], sem_send.at[7])
    settle(stage_x.at[0], sem_send.at[12])
    settle(p_buf.at[:, 0:2], sem_send.at[13])
    settle(s_buf.at[0, 0:7], sem_send.at[8])
    settle(others_rows, sem_send.at[2])
    settle(others_rows, sem_send.at[10])

    @pl.when(has_extra)
    def _():
        settle(rx.at[0, pl.ds(0, (EXTRA - 1) * ROWS), :], sem_send.at[3])
        settle(stage_s.at[0 : 2 * (EXTRA - 1)], sem_send.at[6])
        settle(s_buf.at[1, 0:6], sem_send.at[9])
        settle(others_rows, sem_send.at[11])

    @pl.when(jnp.logical_not(has_extra))
    def _():
        settle(rx.at[0, pl.ds(0, EXTRA * ROWS), :], sem_send.at[3])
        settle(stage_s.at[0 : 2 * EXTRA], sem_send.at[6])

    settle(out, sem_o)


def per_device(grads, panels, eigvals, owner_slot):
    return pl.pallas_call(
        kernel,
        out_shape=jax.ShapeDtypeStruct(grads.shape, BF16),
        in_specs=[
            pl.BlockSpec(memory_space=pltpu.HBM),
            pl.BlockSpec(memory_space=pltpu.HBM),
            pl.BlockSpec(memory_space=pltpu.HBM),
            pl.BlockSpec(memory_space=pltpu.HBM),
        ],
        out_specs=pl.BlockSpec(memory_space=pl.ANY),
        scratch_shapes=[
            pltpu.SMEM(owner_slot.shape, jnp.int32),
            pltpu.VMEM(grads.shape, BF16),
            pltpu.VMEM((SLOTS, N // Q, N), BF16),
            pltpu.VMEM(eigvals.shape, BF16),
            pltpu.VMEM((W * SLOTS, 16, 128), BF16),
            pltpu.VMEM((W, 16, 128), BF16),
            pltpu.VMEM((16, 128), BF16),
            pltpu.VMEM((16, 128), F32),
            pltpu.VMEM((W * SLOTS, 8, 128), F32),
            pltpu.VMEM((W, 16, 128), BF16),
            pltpu.VMEM((16, 128), BF16),
            pltpu.VMEM((W, 16, 128), BF16),
            pltpu.VMEM((2, EXTRA, 16, 128), BF16),
            pltpu.VMEM((Q, 16, 128), BF16),
            pltpu.VMEM((Q, 4, 16, N), BF16),
            pltpu.VMEM((2, Q, 4, 16, N), BF16),
            pltpu.VMEM((2, N, N), BF16),
            pltpu.VMEM((2, 2, N, N // 2), BF16),
            pltpu.VMEM((N, N), BF16),
            pltpu.VMEM((N, N), BF16),
            pltpu.SemaphoreType.DMA((4,)),
            pltpu.SemaphoreType.DMA((15,)),
            pltpu.SemaphoreType.DMA,
            pltpu.SemaphoreType.DMA((2,)),
            pltpu.SemaphoreType.DMA,
            pltpu.SemaphoreType.DMA((8,)),
            pltpu.SemaphoreType.DMA,
            pltpu.SemaphoreType.DMA,
            pltpu.SemaphoreType.DMA((2,)),
            pltpu.SemaphoreType.DMA((2,)),
            pltpu.SemaphoreType.DMA((2,)),
            pltpu.SemaphoreType.DMA,
        ],
        compiler_params=pltpu.CompilerParams(
            collective_id=0, has_side_effects=True, vmem_limit_bytes=32 * 1024 * 1024
        ),
    )(*[pltpu.with_memory_space_constraint(x, pltpu.HBM) for x in (owner_slot, grads, panels, eigvals)])


def solution(mesh):
    return jax.shard_map(
        per_device,
        mesh=mesh,
        in_specs=(P(("rep", "work"), None), P("work", None, None), P("work", None), P()),
        out_specs=P(("rep", "work"), None),
        check_vma=False,
    )
```

```python
import jax
import jax.numpy as jnp
from jax import lax
from jax.experimental import pallas as pl
from jax.experimental.pallas import tpu as pltpu
from jax.sharding import PartitionSpec as P

MESH = pl.DeviceIdType.MESH
N = 512
W = 16
Q = 8
ROWS = 32
RIGHT = 20
LEFT = 16
SLOTS = 4
EXTRA = RIGHT - W
DAMPING = 0.2
BF16 = jnp.bfloat16
F32 = jnp.float32


def partner(w, dx, dz):
    return ((w // 8 + dx) % 2) * 8 + (w % 8 + dz) % 8


def near_first(k):
    return jnp.where(k % 2 == 0, k // 2 + 1, 7 - k // 2)


def extra_home(e, core):
    return (e // 2) * 9 + (e % 2) * 4 + core * 2


def tile(ref, i):
    return ref.at[i // 4, :, pl.ds(pl.multiple_of((i % 4) * 128, 128), 128)]


def kernel(
    owner_hbm, grads_hbm, panels_hbm, eigs_hbm, out,
    owner, grads, panels, eigs,
    tiles, eig_all, eig_mine, eig_f32, eig_slot, eig_out, eig_in,
    stage_s, stage_x, stage_p, p_buf, s_buf, rx, tx, xs, us,
    sem_in, sem_send, sem_t, sem_e, sem_p2, sem_p3, sem_p4, sem_x, sem_s2, sem_s3, sem_g, sem_o,
):
    r = lax.axis_index("rep")
    w = lax.axis_index("work")
    layer = r // Q
    q = r % Q
    core = r % 2
    pair = q - core
    keeper = 2 * q
    extra = jnp.int32(-1)
    for e in range(EXTRA):
        extra = jnp.where(w == extra_home(e, core), e, extra)
    has_extra = extra >= 0
    mine = jnp.where(has_extra, extra, 0)

    barrier = pltpu.get_barrier_semaphore()

    def others_z(body):
        @pl.loop(0, 7)
        def _(k):
            body(partner(w, 0, near_first(k)))

    def others_x(body):
        @pl.loop(0, 7)
        def _(k):
            body(partner(w, 1, near_first(k)))

    def others(body):
        others_z(body)
        body(partner(w, 1, 0))
        others_x(body)

    def mates(body):
        @pl.loop(1, Q)
        def _(k):
            body((q + k) % Q)

    def greet(t):
        pl.semaphore_signal(barrier, inc=1, device_id={"work": t}, device_id_type=MESH)

    def greet_mate(m):
        pl.semaphore_signal(barrier, inc=1, device_id={"rep": layer * Q + m}, device_id_type=MESH)

    for dz in (4, 3, 5, 2, 6, 1, 7, 0):
        greet(partner(w, 1, dz))
        if dz:
            greet(partner(w, 0, dz))
    mates(greet_mate)

    def remote(src, dst, send, recv, **where):
        pltpu.make_async_remote_copy(
            src_ref=src, dst_ref=dst, send_sem=send, recv_sem=recv, device_id=where, device_id_type=MESH
        ).start()

    def local(src, dst, sem):
        pltpu.make_async_copy(src, dst, sem).start()

    def settle(ref, sem):
        pltpu.make_async_copy(ref, ref, sem).wait()

    slab = panels_hbm.at[:, pl.ds(pl.multiple_of(q * 64, 64), 64), :]
    local(slab, panels, sem_in.at[0])
    local(eigs_hbm, eigs, sem_in.at[1])
    local(grads_hbm, grads, sem_in.at[2])
    local(owner_hbm, owner, sem_in.at[3])
    settle(panels, sem_in.at[0])
    pl.semaphore_wait(barrier, W - 1 + Q - 1)

    def piece_of(i):
        rows = pl.multiple_of((i // 4) * 16, 16)
        return panels.at[:, pl.ds(rows, 16), pl.ds(pl.multiple_of((i % 4) * 128, 128), 128)]

    def tiles_out():
        def send_tiles(t):
            remote(piece_of(t), tiles.at[pl.ds(w * SLOTS, SLOTS)], sem_send.at[0], sem_t, work=t)

        for dz in (1, 7, 2, 6, 3, 5, 4):
            send_tiles(partner(w, 0, dz))
        send_tiles(partner(w, 1, 0))
        for dz in (4, 3, 5, 2, 6, 1, 7):
            send_tiles(partner(w, 1, dz))
        local(piece_of(w), tiles.at[pl.ds(w * SLOTS, SLOTS)], sem_t)

    def values_out():
        settle(eigs, sem_in.at[1])

        values = eigs[...].astype(F32)
        for s in range(SLOTS):
            for c in range(4):
                eig_f32[4 * s + c : 4 * s + c + 1, :] = values[s : s + 1, c * 128 : (c + 1) * 128]
        eig_mine[...] = eig_f32[...].astype(BF16)

        @pl.when(w == keeper)
        def _():
            local(eig_mine, eig_all.at[w], sem_e.at[0])

        @pl.when(w != keeper)
        def _():
            remote(eig_mine, eig_all.at[w], sem_send.at[1], sem_e.at[0], work=keeper)

    def block_of(j):
        return grads.at[:, pl.ds(pl.multiple_of(j * N, N), N)]

    def row_slice(ref, u, k):
        return ref.at[u, pl.ds(pl.multiple_of(k * ROWS, ROWS), ROWS), :]

    def send_rows(t):
        remote(block_of(t), row_slice(rx, 0, w), sem_send.at[2], sem_g.at[0], work=t)

    def rows_ready():
        settle(grads, sem_in.at[2])
        rows_own()

    def rows_own():
        local(block_of(w), row_slice(rx, 0, w), sem_g.at[0])

    def rows_to(dx, *steps):
        for dz in steps:
            send_rows(partner(w, dx, dz))

    def rows_extra(a, b):
        @pl.loop(a, b)
        def _(k):
            e = (k + w) % EXTRA
            home = extra_home(e, core)

            @pl.when(home != w)
            def _():
                remote(block_of(W + e), row_slice(rx, 1, w), sem_send.at[3], sem_g.at[1], work=home)

            @pl.when(home == w)
            def _():
                local(block_of(W + e), row_slice(rx, 1, w), sem_g.at[1])

    def p_tile(k):
        return tile(p_buf.at[k], w)

    def left_tiles():
        settle(tiles, sem_t)
        pltpu.make_async_copy(owner_hbm, owner, sem_in.at[3]).wait()

        @pl.loop(0, Q)
        def _(m):
            stage_p[m] = tiles[owner[layer * Q + m]]

        def send_p(m):
            remote(stage_p.at[m], p_tile(q), sem_send.at[4], sem_p2, rep=layer * Q + m)

        mates(send_p)
        local(stage_p.at[q], p_tile(q), sem_p2)

    def extra_tiles_pair():
        @pl.loop(0, EXTRA)
        def _(e):
            stage_x[core, e] = tiles[owner[LEFT + layer * RIGHT + W + e]]

        remote(stage_x.at[core], stage_x.at[core], sem_send.at[12], sem_x, rep=layer * Q + pair + 1 - core)

    def right_tiles():
        @pl.loop(0, W)
        def _(j):
            stage_s[j] = tiles[owner[LEFT + layer * RIGHT + j]]

        def send_s(t):
            remote(stage_s.at[t], tile(s_buf.at[0, q], w), sem_send.at[5], sem_s2.at[0], work=t)

        others_z(send_s)
        send_s(partner(w, 1, 0))
        for dz in (4, 3, 5, 2, 6, 1, 7):
            send_s(partner(w, 1, dz))
        local(stage_s.at[w], tile(s_buf.at[0, q], w), sem_s2.at[0])

    def extra_tiles():
        settle(stage_x.at[0], sem_x)

        def x_tiles():
            return s_buf.at[1, pl.ds(pair, 2), w // 4, :, pl.ds(pl.multiple_of((w % 4) * 128, 128), 128)]

        @pl.loop(0, EXTRA)
        def _(k):
            e = (k + w) % EXTRA
            home = extra_home(e, core)

            @pl.when(home != w)
            def _():
                remote(stage_x.at[:, e], x_tiles(), sem_send.at[6], sem_s2.at[1], work=home)

            @pl.when(home == w)
            def _():
                local(stage_x.at[:, e], x_tiles(), sem_s2.at[1])

    def p_share(k):
        return p_buf.at[:, k // 4, :, pl.ds(pl.multiple_of((k % 4) * 128, 128), 128)]

    def send_across(k):
        remote(p_share(k), p_share(k), sem_send.at[13], sem_p4, work=partner(w, 1, 0))

    def left_shares():
        settle(p_share(w), sem_p2)

        def send_share(t):
            remote(p_share(w), p_share(w), sem_send.at[7], sem_p3.at[w % 8], work=t)

        others_z(send_share)
        send_across(w)

    def right_slabs():
        settle(s_buf.at[0, q], sem_s2.at[0])

        def send_slab(m):
            remote(s_buf.at[0, q], s_buf.at[0, q], sem_send.at[8], sem_s3.at[0], rep=layer * Q + m)

        mates(send_slab)

    def extra_slabs():
        @pl.when(has_extra)
        def _():
            settle(s_buf.at[1, pl.ds(pair, 2)], sem_s2.at[1])

            @pl.loop(1, 4)
            def _(k):
                both = s_buf.at[1, pl.ds(pair, 2)]
                remote(both, both, sem_send.at[9], sem_s3.at[1], rep=layer * Q + (q + 2 * k) % Q)

    def hand_values():
        @pl.when(w == keeper)
        def _():
            settle(eig_all, sem_e.at[0])

            for k in range(W):
                rows = eig_all[k].astype(F32)
                for s in range(SLOTS):
                    eig_slot[k * SLOTS + s, 0:4, :] = rows[4 * s : 4 * s + 4]

            eig_f32[0:4, :] = eig_slot[owner[r], 0:4, :]

            def hand(t):
                second = jnp.int32(0)
                for e in range(EXTRA):
                    second = jnp.where(t == extra_home(e, core), e, second)
                eig_f32[4:8, :] = eig_slot[owner[LEFT + layer * RIGHT + t], 0:4, :]
                eig_f32[8:12, :] = eig_slot[owner[LEFT + layer * RIGHT + W + second], 0:4, :]
                eig_out[t] = eig_f32[...].astype(BF16)

            def send_values(t):
                hand(t)
                remote(eig_out.at[t], eig_in, sem_send.at[14], sem_e.at[1], work=t)

            others(send_values)
            hand(w)
            local(eig_out.at[w], eig_in, sem_e.at[1])

    def pass_on():
        @pl.loop(0, 7)
        def _(k):
            t = partner(w, 0, near_first(k))
            settle(p_share(t), sem_p3.at[t % 8])
            send_across(t)

    tiles_out()
    rows_ready()

    @pl.when(core == 0)
    def _():
        rows_to(1, 0)
        rows_to(1, 1, 7)
        rows_to(1, 2, 6)
        rows_to(1, 3, 5)
        rows_to(1, 4)
        rows_to(0, 1, 7)
        rows_to(0, 2, 6)
        rows_to(0, 3, 5)
        rows_to(0, 4)

    values_out()
    left_tiles()
    extra_tiles_pair()
    right_tiles()
    extra_tiles()
    left_shares()
    hand_values()
    right_slabs()

    @pl.when(core == 1)
    def _():
        rows_to(1, 0)
        rows_to(1, 1, 7)
        rows_to(1, 2, 6)
        rows_to(1, 3, 5)
        rows_to(1, 4)
        rows_to(0, 1, 7)
        rows_to(0, 2, 6)
        rows_to(0, 3, 5)
        rows_to(0, 4)

    pass_on()
    extra_slabs()
    rows_extra(0, 4)

    settle(eig_in, sem_e.at[1])
    values_in = eig_in[...].astype(F32)
    left = values_in[0:4]
    columns = []
    for c in range(4):
        columns.append(jnp.transpose(jnp.broadcast_to(left[c : c + 1], (128, 128))))
    left_columns = jnp.concatenate(columns, axis=0)

    others_rows = rx.at[0, pl.ds(0, (W - 1) * ROWS), :]
    settle(p_buf.at[:, 0:2], sem_p4)

    def compute(u, j):
        settle(rx.at[u], sem_g.at[u])
        p = p_buf[...].reshape(N, N)
        halves = [slice(c * 256, (c + 1) * 256) for c in range(2)]
        for cols in halves:
            xs[:, cols] = lax.dot_general(
                p, rx[u, :, cols], (((0,), (0,)), ((), ())), preferred_element_type=F32
            ).astype(BF16)
        settle(s_buf.at[u, 0 : 7 - u], sem_s3.at[u])
        s = s_buf[u].reshape(N, N)
        right = values_in[4 + 4 * u : 8 + 4 * u]
        for c, cols in enumerate(halves):
            turned = jnp.dot(xs[...], s[:, cols], preferred_element_type=F32)
            outer = [left_columns * right[k : k + 1] for k in (2 * c, 2 * c + 1)]
            us[:, cols] = (turned / (jnp.concatenate(outer, axis=1) + DAMPING)).astype(BF16)
        for c, cols in enumerate(halves):
            xs[:, cols] = lax.dot_general(
                us[...], s[cols], (((1,), (1,)), ((), ())), preferred_element_type=F32
            ).astype(BF16)
            tx[u, c] = jnp.dot(p, xs[:, cols], preferred_element_type=F32).astype(BF16)

            def send_out(t):
                remote(own_rows(t), out_block(t), sem_send.at[10 + u], sem_o, work=t)

            def own_rows(t):
                return tx.at[u, c, pl.ds(pl.multiple_of(t * ROWS, ROWS), ROWS), :]

            def out_block(t):
                return out.at[:, pl.ds(pl.multiple_of(j * N + c * 256, 256), 256)]

            others_z(send_out)
            send_out(partner(w, 1, 0))
            for dz in (4, 3, 5, 2, 6, 1, 7):
                send_out(partner(w, 1, dz))
            local(own_rows(w), out_block(w), sem_o)

    compute(0, w)

    @pl.when(has_extra)
    def _():
        compute(1, W + mine)

    settle(tiles.at[0 : (W - 1) * SLOTS], sem_send.at[0])

    @pl.when(w == keeper)
    def _():
        settle(eig_out.at[0 : W - 1], sem_send.at[14])

    @pl.when(w != keeper)
    def _():
        settle(eig_mine, sem_send.at[1])

    settle(stage_p.at[0 : Q - 1], sem_send.at[4])
    settle(stage_s.at[0 : W - 1], sem_send.at[5])
    settle(rx.at[0, pl.ds(0, 7 * ROWS), :], sem_send.at[7])
    settle(stage_x.at[0], sem_send.at[12])
    settle(p_buf.at[:, 0:2], sem_send.at[13])
    settle(s_buf.at[0, 0:7], sem_send.at[8])
    settle(others_rows, sem_send.at[2])
    settle(others_rows, sem_send.at[10])

    @pl.when(has_extra)
    def _():
        settle(rx.at[0, pl.ds(0, (EXTRA - 1) * ROWS), :], sem_send.at[3])
        settle(stage_s.at[0 : 2 * (EXTRA - 1)], sem_send.at[6])
        settle(s_buf.at[1, 0:6], sem_send.at[9])
        settle(others_rows, sem_send.at[11])

    @pl.when(jnp.logical_not(has_extra))
    def _():
        settle(rx.at[0, pl.ds(0, EXTRA * ROWS), :], sem_send.at[3])
        settle(stage_s.at[0 : 2 * EXTRA], sem_send.at[6])

    settle(out, sem_o)


def per_device(grads, panels, eigvals, owner_slot):
    return pl.pallas_call(
        kernel,
        out_shape=jax.ShapeDtypeStruct(grads.shape, BF16),
        in_specs=[
            pl.BlockSpec(memory_space=pltpu.HBM),
            pl.BlockSpec(memory_space=pltpu.HBM),
            pl.BlockSpec(memory_space=pltpu.HBM),
            pl.BlockSpec(memory_space=pltpu.HBM),
        ],
        out_specs=pl.BlockSpec(memory_space=pl.ANY),
        scratch_shapes=[
            pltpu.SMEM(owner_slot.shape, jnp.int32),
            pltpu.VMEM(grads.shape, BF16),
            pltpu.VMEM((SLOTS, N // Q, N), BF16),
            pltpu.VMEM(eigvals.shape, BF16),
            pltpu.VMEM((W * SLOTS, 16, 128), BF16),
            pltpu.VMEM((W, 16, 128), BF16),
            pltpu.VMEM((16, 128), BF16),
            pltpu.VMEM((16, 128), F32),
            pltpu.VMEM((W * SLOTS, 8, 128), F32),
            pltpu.VMEM((W, 16, 128), BF16),
            pltpu.VMEM((16, 128), BF16),
            pltpu.VMEM((W, 16, 128), BF16),
            pltpu.VMEM((2, EXTRA, 16, 128), BF16),
            pltpu.VMEM((Q, 16, 128), BF16),
            pltpu.VMEM((Q, 4, 16, N), BF16),
            pltpu.VMEM((2, Q, 4, 16, N), BF16),
            pltpu.VMEM((2, N, N), BF16),
            pltpu.VMEM((2, 2, N, N // 2), BF16),
            pltpu.VMEM((N, N), BF16),
            pltpu.VMEM((N, N), BF16),
            pltpu.SemaphoreType.DMA((4,)),
            pltpu.SemaphoreType.DMA((15,)),
            pltpu.SemaphoreType.DMA,
            pltpu.SemaphoreType.DMA((2,)),
            pltpu.SemaphoreType.DMA,
            pltpu.SemaphoreType.DMA((8,)),
            pltpu.SemaphoreType.DMA,
            pltpu.SemaphoreType.DMA,
            pltpu.SemaphoreType.DMA((2,)),
            pltpu.SemaphoreType.DMA((2,)),
            pltpu.SemaphoreType.DMA((2,)),
            pltpu.SemaphoreType.DMA,
        ],
        compiler_params=pltpu.CompilerParams(
            collective_id=0, has_side_effects=True, vmem_limit_bytes=32 * 1024 * 1024
        ),
    )(*[pltpu.with_memory_space_constraint(x, pltpu.HBM) for x in (owner_slot, grads, panels, eigvals)])


def solution(mesh):
    return jax.shard_map(
        per_device,
        mesh=mesh,
        in_specs=(P(("rep", "work"), None), P("work", None, None), P("work", None), P()),
        out_specs=P(("rep", "work"), None),
        check_vma=False,
    )
```
